128 devices in a mesh: row: 8 (over y, core), col: 16 (over z, x).
Axes of the slice: x: 4, y: 4, z: 4, core: 2. Of those that a mesh axis runs over, the one named last changes fastest.
Arguments:
- object_field: float32 [2, 4096, 8192], P(None, 'row', 'col'), may hold values from -6 to 6
- probe: float32 [2, 2, 256, 256], replicated, may hold values from -6 to 6
- patterns: float32 [1024, 256, 256], P(('row', 'col')), may hold values from 0 to 3
- offsets: int32 [1024, 2], P(('row', 'col')), may hold values from 0 to 7936, as said below
Outputs:
- object_grad: float32 [2, 4096, 8192], P(None, 'row', 'col')
- probe_grad: float32 [2, 2, 256, 256], replicated
The draws below stay inside these ranges and needn't reach their ends.
Inputs may be any that keep to these rules, and one draw needn't show every extreme that they name: `offsets`: position p belongs to device p // 8 of the row-major grid of 8 x 16 tiles, and the centre (y + 128, x + 128) of its patch lies in that device's tile of 512 x 512 object cells; every patch lies inside the object. On every device, positions 0 to 3 of its list put the centre as near each of the tile's four corners as the object allows.
All inputs are finite; a program needn't handle non-finite values.
Results may differ from the reference program's by a relative error of at most 0.0001.
Values sent between devices are 32-bit elements; how exact they have to be, the bound alone decides.
A program may use at most 128 MiB of HBM per device.

```python
import jax
import jax.numpy as jnp
from jax import lax

S = 256
MODES = 2
TH = 512
TW = 512
P_DEV = 8
NY = 4096
NX = 8192
POSITIONS = 1024
N_COL = 16


def draw_offsets(key, part):
    key = jax.random.fold_in(key, 11)
    key_rows, key_cols = jax.random.split(key)
    half = S // 2
    number = jnp.arange(POSITIONS, dtype=jnp.int32)
    place = number // P_DEV
    within = number % P_DEV
    tile_row = place // N_COL
    tile_col = place % N_COL
    low_y = jnp.maximum(tile_row * TH - half, 0)
    high_y = jnp.minimum(tile_row * TH + TH - half, NY - S + 1)
    low_x = jnp.maximum(tile_col * TW - half, 0)
    high_x = jnp.minimum(tile_col * TW + TW - half, NX - S + 1)
    rows = jax.random.randint(key_rows, (POSITIONS,), low_y, high_y, dtype=jnp.int32)
    cols = jax.random.randint(key_cols, (POSITIONS,), low_x, high_x, dtype=jnp.int32)
    rows = jnp.where((within == 0) | (within == 1), low_y, rows)
    rows = jnp.where((within == 2) | (within == 3), high_y - 1, rows)
    cols = jnp.where((within == 0) | (within == 2), low_x, cols)
    cols = jnp.where((within == 1) | (within == 3), high_x - 1, cols)
    return jnp.stack([rows, cols], axis=1).astype(jnp.int32)


def shard_levels(own_key, dims, pieces, least, high):
    gain, own = 1.0, jax.random.fold_in(own_key, 6)
    for position, blocks in pieces:
        draws = jnp.exp(jax.random.uniform(jax.random.fold_in(own, position), (blocks,), jnp.float32, least / len(pieces), high / len(pieces)))
        gain = gain * jnp.repeat(draws, dims[position] // blocks).reshape([-1 if axis == position else 1 for axis in range(len(dims))])
    return gain


def centred(rng, shape, scale, bound, pieces=(), kind=jnp.bfloat16):
    level = shard_levels(rng, shape, pieces, -0.22, 0.18) if pieces else 1.0
    entries = jax.random.normal(rng, shape, jnp.float32) * scale * level
    return jnp.minimum(jnp.maximum(entries, -bound), bound).astype(kind)


def setup_inputs(seed: int = 0) -> dict:
    splits = jax.random.split(jax.random.key(seed), 5)
    return {
        "object_field": centred(splits[0], (2, NY, NX), 0.7, 6.0, ((1, 8), (2, 16)), jnp.float32),
        "probe": centred(splits[1], (2, MODES, S, S), 0.7, 6.0, (), jnp.float32),
        "patterns": jnp.clip(3.0 * jax.random.uniform(splits[2], (POSITIONS, S, S), jnp.float32) ** shard_levels(splits[2], (POSITIONS, S, S), ((0, 128),), -0.2, 0.2), 0.0, 3.0),
        "offsets": draw_offsets(jax.random.fold_in(splits[4], 71), 0),
    }


def reference(object_field, probe, patterns, offsets):
    modes = probe[0] + 1j * probe[1]
    zero = jnp.zeros((), jnp.int32)

    def visit(index, carry):
        grad, probe_acc = carry
        corner_y = offsets[index, 0].astype(jnp.int32)
        corner_x = offsets[index, 1].astype(jnp.int32)
        patch = lax.dynamic_slice(object_field, (zero, corner_y, corner_x), (2, S, S))
        cells = patch[0] + 1j * patch[1]
        wave = jnp.fft.fft2(modes * cells[None], norm="ortho")
        misfit = jnp.sum(wave.real * wave.real + wave.imag * wave.imag, axis=0) - patterns[index]
        exit_grad = jnp.fft.ifft2(2.0 * misfit[None] * wave, norm="ortho")
        patch_grad = jnp.sum(jnp.conj(modes) * exit_grad, axis=0)
        mode_grad = jnp.conj(cells)[None] * exit_grad
        current = lax.dynamic_slice(grad, (zero, corner_y, corner_x), (2, S, S))
        update = current + jnp.stack([patch_grad.real, patch_grad.imag])
        grad = lax.dynamic_update_slice(grad, update, (zero, corner_y, corner_x))
        probe_acc = probe_acc + jnp.stack([mode_grad.real, mode_grad.imag])
        return grad, probe_acc

    start = (jnp.zeros(object_field.shape, jnp.float32), jnp.zeros(probe.shape, jnp.float32))
    object_grad, probe_grad = lax.fori_loop(0, POSITIONS, visit, start)
    return object_grad, probe_grad
```

```python
import math, functools
import numpy as np, ml_dtypes
import jax, jax.numpy as jnp
from jax import lax
from jax.experimental import pallas as pl
from jax.experimental.pallas import tpu as pltpu
from jax.sharding import PartitionSpec as P

BF = jnp.bfloat16
F32 = jnp.float32

def split_np(w):
    hi = w.astype(np.float32).astype(ml_dtypes.bfloat16)
    lo = (w - hi.astype(np.float64)).astype(np.float32).astype(ml_dtypes.bfloat16)
    return np.stack([hi, lo])

def tables(n):
    h = n // 2
    a = np.arange(h)
    f = 1.0 / math.sqrt(n)
    out = []
    for par in (0, 1):
        c = np.exp(-2j * np.pi * np.outer(a, 2 * a + par) / n) * f
        fwd = np.block([[c.real, c.imag], [-c.imag, c.real]])
        inv_c = np.conj(c).T
        inv = np.block([[inv_c.real, inv_c.imag], [-inv_c.imag, inv_c.real]])
        out.append((fwd, inv))
    rf = np.stack([split_np(out[p][0]) for p in (0, 1)])
    ri = np.stack([split_np(out[p][1]) for p in (0, 1)])
    cf = np.stack([split_np(out[p][0].T) for p in (0, 1)])
    ci = np.stack([split_np(out[p][1].T) for p in (0, 1)])
    perm = np.zeros((n, n), np.float32)
    for k in range(h):
        perm[2 * k, k] = 1
        perm[2 * k + 1, h + k] = 1
    return rf, cf, ci, ri, perm.astype(ml_dtypes.bfloat16)

def split(x):
    hi = x.astype(BF)
    lo = (x - hi.astype(F32)).astype(BF)
    return hi, lo

def rdot(x, w):
    hi, lo = split(x)
    lhs = jnp.concatenate([hi, lo, hi], axis=1)
    rhs = jnp.concatenate([w[0], w[0], w[1]], axis=0)
    return jnp.dot(lhs, rhs, preferred_element_type=F32)

def cdot(w, x):
    hi, lo = split(x)
    lhs = jnp.concatenate([w[0], w[0], w[1]], axis=1)
    rhs = jnp.concatenate([hi, lo, hi], axis=0)
    return jnp.dot(lhs, rhs, preferred_element_type=F32)

def kernel(off_ref, ext_ref, probe_ref, pat_ref, rf, cf, ci, ri, perm, acc_ref, pg_ref, patch, wave, pscr, S=256):
    H = 128
    p = pl.program_id(0)
    y = off_ref[p, 0]
    x = off_ref[p, 1]
    j0 = jnp.minimum(lax.shift_right_logical(x, 7), 3)
    s = x - j0 * 128
    lane = lax.broadcasted_iota(jnp.int32, (S, 128), 1)

    @pl.when(p == 0)
    def _():
        acc_ref[...] = jnp.zeros_like(acc_ref)
        pg_ref[...] = jnp.zeros_like(pg_ref)

    back = jnp.where(s == 0, 0, 128 - s) & 127
    for c in range(2):
        r = [pltpu.roll(ext_ref[c, j0 + k, pl.ds(y, S), :], back, 1) for k in range(3)]
        for k in range(2):
            patch[c, :, k * 128:(k + 1) * 128] = jnp.where(lane < 128 - s, r[k], r[k + 1])

    for m in range(2):
        ar, ai = patch[0], patch[1]
        pr, pi_ = probe_ref[0, m], probe_ref[1, m]
        er = pr * ar - pi_ * ai
        ei = pr * ai + pi_ * ar
        e = jnp.concatenate([er[:, :H] + er[:, H:], ei[:, :H] + ei[:, H:]], axis=1)
        o = jnp.concatenate([er[:, :H] - er[:, H:], ei[:, :H] - ei[:, H:]], axis=1)
        te = rdot(e, rf.at[0])
        to = rdot(o, rf.at[1])
        R = jnp.concatenate([te[:, :H], to[:, :H]], axis=1)
        I = jnp.concatenate([te[:, H:], to[:, H:]], axis=1)
        e2 = jnp.concatenate([R[:H] + R[H:], I[:H] + I[H:]], axis=0)
        o2 = jnp.concatenate([R[:H] - R[H:], I[:H] - I[H:]], axis=0)
        wave[m, 0] = cdot(cf.at[0], e2)
        wave[m, 1] = cdot(cf.at[1], o2)
    hi, lo = split(pat_ref[0])
    pv = jnp.dot(hi, perm[...], preferred_element_type=F32) + jnp.dot(lo, perm[...], preferred_element_type=F32)
    for k in range(2):
        pscr[k] = pv[:, k * H:(k + 1) * H]
    pp = [jnp.concatenate([pscr[k, pl.ds(q, H, stride=2), :] for k in range(2)], axis=1) for q in range(2)]
    for q in range(2):
        inten = sum(wave[m, q, :H] * wave[m, q, :H] + wave[m, q, H:] * wave[m, q, H:] for m in range(2))
        mis = 2.0 * (inten - pp[q])
        for m in range(2):
            wave[m, q, :H] = wave[m, q, :H] * mis
            wave[m, q, H:] = wave[m, q, H:] * mis
    gsum = [None, None]
    for m in range(2):
        A = cdot(ci.at[0], wave[m, 0])
        B = cdot(ci.at[1], wave[m, 1])
        top, bot = A + B, A - B
        R = jnp.concatenate([top[:H], bot[:H]], axis=0)
        I = jnp.concatenate([top[H:], bot[H:]], axis=0)
        A = rdot(jnp.concatenate([R[:, :H], I[:, :H]], axis=1), ri.at[0])
        B = rdot(jnp.concatenate([R[:, H:], I[:, H:]], axis=1), ri.at[1])
        l, r = A + B, A - B
        gr = jnp.concatenate([l[:, :H], r[:, :H]], axis=1)
        gi = jnp.concatenate([l[:, H:], r[:, H:]], axis=1)
        ar, ai = patch[0], patch[1]
        pr, pi_ = probe_ref[0, m], probe_ref[1, m]
        for k in range(2):
            cols = slice(k * H, k * H + H)
            at = slice(k * S, k * S + S)
            pg_ref[0, m, at] += ar[:, cols] * gr[:, cols] + ai[:, cols] * gi[:, cols]
            pg_ref[1, m, at] += ar[:, cols] * gi[:, cols] - ai[:, cols] * gr[:, cols]
        a = pr * gr + pi_ * gi
        b = pr * gi - pi_ * gr
        gsum = [a, b] if m == 0 else [gsum[0] + a, gsum[1] + b]
    for c in range(2):
        g = [pltpu.roll(gsum[c][:, k * 128:(k + 1) * 128], s & 127, 1) for k in range(2)]
        blocks = [jnp.where(lane >= s, g[0], 0.0), jnp.where(lane >= s, g[1], g[0]), jnp.where(lane >= s, 0.0, g[1])]
        for k in range(3):
            acc_ref[c, j0 + k, pl.ds(y, S), :] += blocks[k]

def compute(ext, probe, patterns, local):
    P_, S, _ = patterns.shape
    rf, cf, ci, ri, perm = tables(S)
    full = lambda shape: pl.BlockSpec(shape, lambda p: (0,) * len(shape))
    return pl.pallas_call(
        functools.partial(kernel, S=S),
        grid=(P_,),
        out_shape=(jax.ShapeDtypeStruct(ext.shape, F32), jax.ShapeDtypeStruct((2, 2, 512, 128), F32)),
        in_specs=[pl.BlockSpec(memory_space=pltpu.SMEM), full(ext.shape), full(probe.shape),
                  pl.BlockSpec((1, S, S), lambda p: (p, 0, 0)),
                  full(rf.shape), full(cf.shape), full(ci.shape), full(ri.shape), full(perm.shape)],
        out_specs=(full(ext.shape), full((2, 2, 512, 128))),
        scratch_shapes=[pltpu.VMEM((2, S, S), F32), pltpu.VMEM((2, 2, S, S), F32), pltpu.VMEM((2, S, 128), F32)],
        compiler_params=pltpu.CompilerParams(vmem_limit_bytes=56 * 2**20),
    )(local, ext, probe, patterns, *(jnp.asarray(t) for t in (rf, cf, ci, ri, perm)))


MESH = pl.DeviceIdType.MESH


def neighbours():
    rows, cols = lax.axis_size("row"), lax.axis_size("col")
    r, c = lax.axis_index("row"), lax.axis_index("col")
    left = (r, lax.rem(c + cols - 1, cols))
    right = (r, lax.rem(c + 1, cols))
    up = (lax.rem(r + rows - 1, rows), c)
    down = (lax.rem(r + 1, rows), c)
    return left, right, up, down


def meet(devices):
    barrier = pltpu.get_barrier_semaphore()
    for device in devices:
        pl.semaphore_signal(barrier, inc=1, device_id=device, device_id_type=MESH)
    pl.semaphore_wait(barrier, len(devices))


class Sender:
    def __init__(self, send_sem, recv_sem):
        self.send_sem, self.recv_sem, self.copies = send_sem, recv_sem, []

    def __call__(self, src, dst, device):
        n = len(self.copies)
        copy = pltpu.make_async_remote_copy(
            src_ref=src, dst_ref=dst, send_sem=self.send_sem.at[n], recv_sem=self.recv_sem.at[n],
            device_id=device, device_id_type=MESH)
        copy.start()
        self.copies.append(copy)
        return copy

    def finish(self):
        for copy in self.copies:
            copy.wait_send()


def halo_kernel(obj, ext, local_sem, send_sem, recv_sem):
    left, right, up, down = neighbours()
    own = [pltpu.make_async_copy(obj.at[:, :, pl.ds(128 * j, 128)], ext.at[:, 1 + j, pl.ds(128, 512), :], local_sem.at[j])
           for j in range(4)]
    meet((left, right, up, down))
    send = Sender(send_sem, recv_sem)
    across = []
    for start, size in ((0, 128), (384, 128), (128, 256)):
        rows = pl.ds(start, size)
        to = pl.ds(128 + start, size)
        across.append((send(obj.at[:, rows, pl.ds(0, 128)], ext.at[:, 5, to, :], left),
                       send(obj.at[:, rows, pl.ds(384, 128)], ext.at[:, 0, to, :], right)))
    along = []
    for j in range(4):
        block = pl.ds(128 * j, 128)
        along.append(send(obj.at[:, pl.ds(0, 128), block], ext.at[:, 1 + j, pl.ds(640, 128), :], up))
        along.append(send(obj.at[:, pl.ds(384, 128), block], ext.at[:, 1 + j, pl.ds(0, 128), :], down))
    for copy in own:
        copy.start()
    for k, (place, target, device) in enumerate(((128, 640, up), (512, 0, down))):
        for side, copy in zip((5, 0), across[k]):
            copy.wait_recv()
            along.append(send(ext.at[:, side, pl.ds(place, 128), :], ext.at[:, side, pl.ds(target, 128), :], device))
    for copy in across[2]:
        copy.wait_recv()
    for copy in along:
        copy.wait_recv()
    for copy in own:
        copy.wait()
    send.finish()


def halo(object_field):
    return pl.pallas_call(
        halo_kernel,
        out_shape=jax.ShapeDtypeStruct((2, 6, 768, 128), F32),
        in_specs=[pl.BlockSpec(memory_space=pl.ANY)],
        out_specs=pl.BlockSpec(memory_space=pltpu.VMEM),
        scratch_shapes=[pltpu.SemaphoreType.DMA((4,)), pltpu.SemaphoreType.DMA((18,)), pltpu.SemaphoreType.DMA((18,))],
        compiler_params=pltpu.CompilerParams(collective_id=0, has_side_effects=True, vmem_limit_bytes=16 * 2**20),
    )(object_field)


def peers():
    r, c = lax.axis_index("row"), lax.axis_index("col")
    y, core = lax.div(r, 2), lax.rem(r, 2)
    z, x = lax.div(c, 4), lax.rem(c, 4)
    step = lambda i, d: lax.rem(i + d, 4)
    return core, {
        "z": (z, lambda d: (r, step(z, d) * 4 + x)),
        "y": (y, lambda d: (step(y, d) * 2 + core, c)),
        "x": (x, lambda d: (r, z * 4 + step(x, d))),
    }


ORDERS = (("z", "y", "x"), ("y", "z", "x"))
SIZES = (128, 32, 8)


def gather_kernel(acc, pg, out, probe_out, ytop, ybot, xl, xr, corner, pair, part, r1, r2, r3, s1, s2, g1, g2, g3, send_sem, recv_sem):
    left, right, up, down = neighbours()
    core, rings = peers()
    r, c = lax.axis_index("row"), lax.axis_index("col")
    other = (r + 1 - 2 * core, c)
    meet((left, right, up, down, other) + tuple(rings[a][1](d) for a in "zyx" for d in (1, 2, 3)))
    send = Sender(send_sem, recv_sem)
    paired = send(pg.at[1 - core], pair, other)
    sides = []
    for side in (0, 5):
        sides.append((send(acc.at[:, side, pl.ds(0, 128), :], ybot.at[:, side], up),
                      send(acc.at[:, side, pl.ds(640, 128), :], ytop.at[:, side], down)))
    middle = (send(acc.at[:, 0, pl.ds(256, 256), :], xr.at[:, pl.ds(128, 256), :], left),
              send(acc.at[:, 5, pl.ds(256, 256), :], xl.at[:, pl.ds(128, 256), :], right))
    along = (send(acc.at[:, pl.ds(1, 4), pl.ds(0, 128), :], ybot.at[:, pl.ds(1, 4)], up),
             send(acc.at[:, pl.ds(1, 4), pl.ds(640, 128), :], ytop.at[:, pl.ds(1, 4)], down))

    def scatter(q, stage, src, dst):
        place, device = rings[ORDERS[q][stage]]
        size = SIZES[stage]
        return [send(src.at[pl.ds(pl.multiple_of(lax.rem(place + d, 4) * size, 8), size), :], dst.at[d - 1], device(d)) for d in (1, 2, 3)]

    def reduced(q, stage, src, got, copies):
        place, _ = rings[ORDERS[q][stage]]
        size = SIZES[stage]
        for copy in copies:
            copy.wait_recv()
        return src[pl.ds(pl.multiple_of(place * size, 8), size), :] + got[0] + got[1] + got[2]

    def spread(q, stage, full):
        place, device = rings[ORDERS[q][stage]]
        size = SIZES[stage]
        own = full.at[pl.ds(pl.multiple_of(place * size, 8), size), :]
        return [send(own, own, device(d)) for d in (1, 2, 3)]

    def put(q, stage, full, value):
        place, _ = rings[ORDERS[q][stage]]
        size = SIZES[stage]
        full[pl.ds(pl.multiple_of(place * size, 8), size), :] = value

    paired.wait_recv()
    first = []
    for q in range(2):
        part[q] = pg[core, q] + pair[q]
        first.append(scatter(q, 0, part.at[q], r1.at[q]))

    corners = []
    for side, (from_down, from_up) in zip((0, 5), sides):
        from_down.wait_recv()
        from_up.wait_recv()
        for n, (at, got) in enumerate(((128, ytop), (512, ybot))):
            held = corner.at[side % 2, n]
            for ch in range(2):
                corner[side % 2, n, ch] = acc[ch, side, at:at + 128] + got[ch, side]
            to = pl.ds(at - 128, 128)
            corners.append(send(held, (xr if side == 0 else xl).at[:, to, :], left if side == 0 else right))

    second = []
    for q in range(2):
        s1[q] = reduced(q, 0, part.at[q], r1.at[q], first[q])
        second.append(scatter(q, 1, s1.at[q], r2.at[q]))
    third = []
    for q in range(2):
        s2[q] = reduced(q, 1, s1.at[q], r2.at[q], second[q])
        third.append(scatter(q, 2, s2.at[q], r3.at[q]))
    back3 = []
    for q in range(2):
        put(q, 2, g3.at[q], reduced(q, 2, s2.at[q], r3.at[q], third[q]))
        back3.append(spread(q, 2, g3.at[q]))
    back2 = []
    for q in range(2):
        for copy in back3[q]:
            copy.wait_recv()
        put(q, 1, g2.at[q], g3[q])
        back2.append(spread(q, 1, g2.at[q]))
    back1 = []
    for q in range(2):
        for copy in back2[q]:
            copy.wait_recv()
        put(q, 0, g1.at[core, q], g2[q])
        back1.append(spread(q, 0, g1.at[core, q]))
    last = []
    for q in range(2):
        for copy in back1[q]:
            copy.wait_recv()
        last.append(send(g1.at[core, q], g1.at[core, q], other))

    for copy in along:
        copy.wait_recv()
    for copy in middle:
        copy.wait_recv()
    for copy in corners:
        copy.wait_recv()
    for ch in range(2):
        for j in range(4):
            extra = xl if j == 0 else xr if j == 3 else None
            for start, size, more in ((0, 128, ytop), (128, 256, None), (384, 128, ybot)):
                value = acc[ch, 1 + j, 128 + start:128 + start + size]
                if more is not None:
                    value = value + more[ch, 1 + j]
                if extra is not None:
                    value = value + extra[ch, start:start + size]
                out[ch, start:start + size, 128 * j:128 * j + 128] = value
    for copy in last:
        copy.wait_recv()
    for h in range(2):
        for q in range(2):
            for k in range(2):
                probe_out[h, q, :, 128 * k:128 * k + 128] = g1[h, q, 256 * k:256 * k + 256]
    send.finish()


def finish(acc, pg):
    V = lambda *shape: pltpu.VMEM(shape, F32)
    count = 1 + 4 + 2 + 2 + 6 + 4 + 6 + 6 + 18 + 2
    return pl.pallas_call(
        gather_kernel,
        out_shape=(jax.ShapeDtypeStruct((2, 512, 512), F32), jax.ShapeDtypeStruct((2, 2, 256, 256), F32)),
        in_specs=[pl.BlockSpec(memory_space=pltpu.VMEM)] * 2,
        out_specs=(pl.BlockSpec(memory_space=pltpu.VMEM),) * 2,
        scratch_shapes=[V(2, 6, 128, 128), V(2, 6, 128, 128), V(2, 512, 128), V(2, 512, 128), V(2, 2, 2, 128, 128), V(2, 512, 128), V(2, 512, 128),
                        V(2, 3, 128, 128), V(2, 3, 32, 128), V(2, 3, 8, 128), V(2, 128, 128), V(2, 32, 128),
                        V(2, 2, 512, 128), V(2, 128, 128), V(2, 32, 128),
                        pltpu.SemaphoreType.DMA((count,)), pltpu.SemaphoreType.DMA((count,))],
        compiler_params=pltpu.CompilerParams(collective_id=1, has_side_effects=True, vmem_limit_bytes=40 * 2**20),
    )(acc, pg)


def body(object_field, probe, patterns, offsets):
    base = jnp.stack([lax.axis_index("row") * 512 - 128, lax.axis_index("col") * 512 - 128])
    ext = halo(object_field)
    acc, pg = compute(ext, probe, patterns, offsets - base[None, :])
    return finish(acc, pg)


def solution(mesh):
    in_specs = (P(None, "row", "col"), P(), P(("row", "col"), None, None), P(("row", "col"), None))
    out_specs = (P(None, "row", "col"), P())
    return jax.shard_map(body, mesh=mesh, in_specs=in_specs, out_specs=out_specs, check_vma=False)
```

```python
import functools
import math

import jax
import jax.numpy as jnp
import ml_dtypes
import numpy as np
from jax import lax
from jax.experimental import pallas as pl
from jax.experimental.pallas import tpu as pltpu
from jax.sharding import PartitionSpec as P

BF = jnp.bfloat16
F32 = jnp.float32
H = 128
S = 256
MESH = pl.DeviceIdType.MESH

def split_np(w):
    hi = w.astype(np.float32).astype(ml_dtypes.bfloat16)
    lo = (w - hi.astype(np.float64)).astype(np.float32).astype(ml_dtypes.bfloat16)
    return np.stack([hi, lo])

def tables(n):
    h = n // 2
    a = np.arange(h)
    f = 1.0 / math.sqrt(n)
    out = []
    for par in (0, 1):
        c = np.exp(-2j * np.pi * np.outer(a, 2 * a + par) / n) * f
        fwd = np.block([[c.real, c.imag], [-c.imag, c.real]])
        inv_c = np.conj(c).T
        inv = np.block([[inv_c.real, inv_c.imag], [-inv_c.imag, inv_c.real]])
        out.append((fwd, inv))
    rf = np.stack([split_np(out[p][0]) for p in (0, 1)])
    ri = np.stack([split_np(out[p][1]) for p in (0, 1)])
    cf = np.stack([split_np(out[p][0].T) for p in (0, 1)])
    ci = np.stack([split_np(out[p][1].T) for p in (0, 1)])
    perm = np.zeros((n, n), np.float32)
    for k in range(h):
        perm[2 * k, k] = 1
        perm[2 * k + 1, h + k] = 1
    return rf, cf, ci, ri, perm.astype(ml_dtypes.bfloat16)

def split(x):
    hi = x.astype(BF)
    lo = (x - hi.astype(F32)).astype(BF)
    return hi, lo


def run(steps):
    for mxu, vpu in steps:
        n = max(len(mxu), 1)
        for i in range(n):
            if i < len(mxu):
                mxu[i]()
            for t in vpu[len(vpu) * i // n: len(vpu) * (i + 1) // n]:
                t()

class Work:
    def __init__(self, **refs):
        self.__dict__.update(refs)

    def rows_dot(self, lhs, table, out):
        l = lhs[...]
        t0, t1 = table[0], table[1]
        out[...] = jnp.dot(jnp.concatenate([l, l[:, :S]], axis=1), jnp.concatenate([t0, t0, t1], axis=0), preferred_element_type=F32)

    def cols_dot(self, table, rhs, out):
        r = rhs[...]
        t0, t1 = table[0], table[1]
        out[...] = jnp.dot(jnp.concatenate([t0, t0, t1], axis=1), jnp.concatenate([r, r[:S]], axis=0), preferred_element_type=F32)

    def s1(self, m): return [lambda q=q: self.rows_dot(self.lhs1.at[m, q], self.rf.at[q], self.o1.at[m, q]) for q in range(2)]
    def s2(self, m): return [lambda q=q: self.cols_dot(self.cf.at[q], self.rhs2.at[m, q], self.o2.at[m, q]) for q in range(2)]
    def s3(self, m): return [lambda q=q: self.cols_dot(self.ci.at[q], self.rhs3.at[m, q], self.o3.at[m, q]) for q in range(2)]
    def s4(self, m): return [lambda q=q: self.rows_dot(self.lhs4.at[m, q], self.ri.at[q], self.o4.at[m, q]) for q in range(2)]

    def put_row(self, ref, rows, re, im):
        hi, lo = split(re)
        ref[rows, 0:H] = hi
        ref[rows, S:S + H] = lo
        hi, lo = split(im)
        ref[rows, H:S] = hi
        ref[rows, S + H:2 * S] = lo

    def put_col(self, ref, row, size, re, im):
        hi, lo = split(re)
        ref[row:row + size] = hi
        ref[S + row:S + row + size] = lo
        hi, lo = split(im)
        ref[H + row:H + row + size] = hi
        ref[S + H + row:S + H + row + size] = lo

    def v1(self, m, slot, size=16):
        def chunk(a):
            rows = slice(a, a + size)
            ar, ai = self.patch[slot, 0, rows], self.patch[slot, 1, rows]
            pr, pi_ = self.probe[0, m, rows], self.probe[1, m, rows]
            er = pr * ar - pi_ * ai
            ei = pr * ai + pi_ * ar
            self.put_row(self.lhs1.at[m, 0], rows, er[:, :H] + er[:, H:], ei[:, :H] + ei[:, H:])
            self.put_row(self.lhs1.at[m, 1], rows, er[:, :H] - er[:, H:], ei[:, :H] - ei[:, H:])
        return [functools.partial(chunk, a) for a in range(0, S, size)]

    def v2(self, m, size=16):
        def chunk(a):
            top, bot = slice(a, a + size), slice(H + a, H + a + size)
            for q in range(2):
                t, b = self.o1[m, q, top], self.o1[m, q, bot]
                p, n = t + b, t - b
                cols = slice(q * H, q * H + H)
                for par, v in ((0, p), (1, n)):
                    self.put_col(self.rhs2.at[m, par, :, cols], a, size, v[:, :H], v[:, H:])
        return [functools.partial(chunk, a) for a in range(0, H, size)]

    def vp(self, number):
        def first():
            hi, lo = split(self.pat[number])
            w = self.perm[...]
            v = jnp.dot(jnp.concatenate([hi, lo], axis=1), jnp.concatenate([w, w], axis=0), preferred_element_type=F32)
            for k in range(2):
                self.pscr[k] = v[:, k * H:(k + 1) * H]
        return [first]

    def v3(self, size=16):
        def chunk(q, a):
            re, im = slice(a, a + size), slice(H + a, H + a + size)
            w = [(self.o2[m, q, re], self.o2[m, q, im]) for m in range(2)]
            inten = w[0][0] * w[0][0] + w[0][1] * w[0][1] + w[1][0] * w[1][0] + w[1][1] * w[1][1]
            pat = jnp.concatenate([self.pscr[k, pl.ds(q + 2 * a, size, stride=2), :] for k in range(2)], axis=1)
            mis = 2.0 * (inten - pat)
            for m in range(2):
                self.put_col(self.rhs3.at[m, q], a, size, w[m][0] * mis, w[m][1] * mis)
        return [functools.partial(chunk, q, a) for q in range(2) for a in range(0, H, size)]

    def v4(self, m, size=16):
        def chunk(a):
            for at, op in ((a, lambda x, y: x + y), (H + a, lambda x, y: x - y)):
                re = op(self.o3[m, 0, a:a + size], self.o3[m, 1, a:a + size])
                im = op(self.o3[m, 0, H + a:H + a + size], self.o3[m, 1, H + a:H + a + size])
                for q in range(2):
                    cols = slice(q * H, q * H + H)
                    self.put_row(self.lhs4.at[m, q], slice(at, at + size), re[:, cols], im[:, cols])
        return [functools.partial(chunk, a) for a in range(0, H, size)]

    def v5(self, m, slot, size=8):
        def chunk(a):
            rows = slice(a, a + size)
            A, B = self.o4[m, 0, rows], self.o4[m, 1, rows]
            both = (A + B, A - B)
            for k in range(2):
                cols = slice(k * H, k * H + H)
                gr, gi = both[k][:, :H], both[k][:, H:]
                ar, ai = self.patch[slot, 0, rows, cols], self.patch[slot, 1, rows, cols]
                pr, pi_ = self.probe[0, m, rows, cols], self.probe[1, m, rows, cols]
                at = slice(k * S + a, k * S + a + size)
                self.pg[0, m, at] += ar * gr + ai * gi
                self.pg[1, m, at] += ar * gi - ai * gr
                re = pr * gr + pi_ * gi
                im = pr * gi - pi_ * gr
                if m == 0:
                    self.gsum[0, k, rows] = re
                    self.gsum[1, k, rows] = im
                else:
                    self.gsum[0, k, rows] += re
                    self.gsum[1, k, rows] += im
        return [functools.partial(chunk, a) for a in range(0, S, size)]

    def gather(self, slot, y, x):
        j0 = jnp.minimum(lax.shift_right_logical(x, 7), 3)
        s = x - j0 * 128
        back = (128 - s) & 127
        lane = lax.broadcasted_iota(jnp.int32, (32, 128), 1)
        for c in range(2):
            for a in range(0, S, 32):
                r = [pltpu.roll(self.ext[c, j0 + k, pl.ds(y + a, 32), :], back, 1) for k in range(3)]
                for k in range(2):
                    self.patch[slot, c, a:a + 32, k * 128:(k + 1) * 128] = jnp.where(lane < 128 - s, r[k], r[k + 1])

    def shifted(self, a, s):
        lane = lax.broadcasted_iota(jnp.int32, (32, 128), 1)
        for c in range(2):
            g = [pltpu.roll(self.gsum[c, k, a:a + 32], s & 127, 1) for k in range(2)]
            yield c, (jnp.where(lane >= s, g[0], 0.0), jnp.where(lane >= s, g[1], g[0]), jnp.where(lane >= s, 0.0, g[1]))

    def deposit(self, y, x):
        j0, s = column(x)
        for a in range(0, S, 32):
            for c, blocks in self.shifted(a, s):
                for k in range(3):
                    self.acc[c, j0 + k, pl.ds(y + a, 32), :] += blocks[k]

    def keep(self, number, x):
        j0, s = column(x)
        for a in range(0, S, 32):
            for c, blocks in self.shifted(a, s):
                for k in range(3):
                    self.held[number, c, 1 + k, PAD + a:PAD + a + 32] = blocks[k]

    def merge(self, places, block, start, size):
        def go(t, carry):
            row = pl.multiple_of(start + t * 32, 32)
            for c in range(2):
                value = self.acc[c, block, pl.ds(row, 32), :]
                for n, (y, j0) in enumerate(places):
                    k = block - j0
                    k = jnp.where((k >= 0) & (k <= 2), k + 1, 0)
                    at = jnp.clip(row - y + PAD, 0, S + PAD)
                    value += self.held[n, c, k, pl.ds(at, 32), :]
                self.acc[c, block, pl.ds(row, 32), :] = value
            return carry
        lax.fori_loop(0, size // 32, go, 0)


PAD = 32


def column(x):
    j0 = jnp.minimum(lax.shift_right_logical(x, 7), 3)
    return j0, x - j0 * 128


def neighbours():
    rows, cols = lax.axis_size("row"), lax.axis_size("col")
    r, c = lax.axis_index("row"), lax.axis_index("col")
    left = (r, lax.rem(c + cols - 1, cols))
    right = (r, lax.rem(c + 1, cols))
    up = (lax.rem(r + rows - 1, rows), c)
    down = (lax.rem(r + 1, rows), c)
    return left, right, up, down


def greet(devices):
    barrier = pltpu.get_barrier_semaphore()
    for device in devices:
        pl.semaphore_signal(barrier, inc=1, device_id=device, device_id_type=MESH)


def met(devices):
    pl.semaphore_wait(pltpu.get_barrier_semaphore(), len(devices))


class Sender:
    def __init__(self, send_sem, recv_sem):
        self.send_sem, self.recv_sem, self.copies = send_sem, recv_sem, []

    def __call__(self, src, dst, device):
        n = len(self.copies)
        copy = pltpu.make_async_remote_copy(
            src_ref=src, dst_ref=dst, send_sem=self.send_sem.at[n], recv_sem=self.recv_sem.at[n],
            device_id=device, device_id_type=MESH)
        copy.start()
        self.copies.append(copy)
        return copy

    def finish(self):
        for copy in self.copies:
            copy.wait_send()


class Local:
    def __init__(self, sem):
        self.sem, self.count = sem, 0

    def __call__(self, src, dst):
        copy = pltpu.make_async_copy(src, dst, self.sem.at[self.count])
        self.count += 1
        copy.start()
        return copy


def arrived(copies):
    for copy in copies:
        copy.wait_recv()


PIECE = 64
SCRATCH = dict(
    ext=((2, 6, 768, H), F32), acc=((2, 6, 768, H), F32), probe=((2, 2, S, S), F32), pat=((8, S, S), F32),
    rf=((2, 2, S, S), BF), cf=((2, 2, S, S), BF), ci=((2, 2, S, S), BF), ri=((2, 2, S, S), BF), perm=((S, S), BF),
    pg=((2, 2, 512, H), F32), patch=((4, 2, S, S), F32), lhs1=((2, 2, S, 2 * S), BF), o1=((2, 2, S, S), F32), rhs2=((2, 2, 2 * S, S), BF),
    o2=((2, 2, S, S), F32), rhs3=((2, 2, 2 * S, S), BF), o3=((2, 2, S, S), F32), lhs4=((2, 2, S, 2 * S), BF), o4=((2, 2, S, S), F32),
    pscr=((2, S, H), F32), gsum=((2, 2, S, H), F32), held=((4, 2, 4, S + 2 * PAD, H), F32),
    ytop=((2, 6, H, H), F32), ybot=((2, 6, H, H), F32), xl=((2, 512, H), F32), xr=((2, 512, H), F32),
    pair=((2, 512, H), F32), part=((1024, H), F32), r1=((15, PIECE, H), F32), r2=((4, PIECE, H), F32), full=((2, 1024, H), F32))
REMOTES = 18 + 1 + 4 + 2 + 15 + 2 + 4 + 3 + 15 + 1
LOCALS = 4 + 7 + 4 + 8


def kernel(off, obj, probe_in, pat_in, rf_in, cf_in, ci_in, ri_in, perm_in, out, probe_out, *scr):
    refs = dict(zip(SCRATCH, scr))
    w = Work(**refs)
    ext, acc, pg = w.ext, w.acc, w.pg
    local_sem, send_sem, recv_sem = scr[len(SCRATCH):]
    r, c = lax.axis_index("row"), lax.axis_index("col")
    rows, cols = lax.axis_size("row"), lax.axis_size("col")
    y, core, z, x = lax.div(r, 2), lax.rem(r, 2), lax.div(c, 4), lax.rem(c, 4)
    left, right, up, down = neighbours()
    other = (r + 1 - 2 * core, c)
    turn = lambda i, d: lax.rem(i + d, 4)
    plane = [(turn(y, a), turn(z, b)) for a in range(4) for b in range(4) if a or b]
    planes = [(a * 2 + core, b * 4 + x) for a, b in plane]
    line = [(r, z * 4 + turn(x, d)) for d in (1, 2, 3)]
    everyone = [left, right, up, down, other] + planes + line
    greet(everyone)
    local = Local(local_sem)
    own = [local(obj.at[:, :, pl.ds(128 * j, 128)], ext.at[:, 1 + j, pl.ds(128, 512), :]) for j in range(4)]
    own += [local(a, b) for a, b in ((probe_in, w.probe), (rf_in, w.rf), (cf_in, w.cf), (perm_in, w.perm), (pat_in, w.pat), (ci_in, w.ci), (ri_in, w.ri))]
    met(everyone)
    send = Sender(send_sem, recv_sem)
    across = []
    for start, size in ((376, 136), (0, 128), (128, 248)):
        tile = pl.ds(start, size)
        to = pl.ds(128 + start, size)
        across.append((send(obj.at[:, tile, pl.ds(0, 128)], ext.at[:, 5, to, :], left),
                       send(obj.at[:, tile, pl.ds(384, 128)], ext.at[:, 0, to, :], right)))
        if start == 376:
            top = [send(obj.at[:, pl.ds(384, 128), pl.ds(128 * j, 128)], ext.at[:, 1 + j, pl.ds(0, 128), :], down) for j in range(4)]
        if start == 0:
            bottom = [send(obj.at[:, pl.ds(0, 128), pl.ds(128 * j, 128)], ext.at[:, 1 + j, pl.ds(640, 128), :], up) for j in range(4)]

    acc[...] = jnp.zeros_like(acc)
    pg[...] = jnp.zeros_like(pg)
    w.o4[...] = jnp.zeros_like(w.o4)
    w.patch[3] = jnp.zeros((2, S, S), F32)
    w.held[:, :, 0] = jnp.zeros((4, 2, S + 2 * PAD, H), F32)
    w.held[:, :, 1:4, 0:PAD] = jnp.zeros((4, 2, 3, PAD, H), F32)
    w.held[:, :, 1:4, S + PAD:] = jnp.zeros((4, 2, 3, PAD, H), F32)

    for k, (place, target, device, group) in enumerate(((512, 0, down, top), (128, 640, up, bottom))):
        for side, copy in zip((5, 0), across[k]):
            copy.wait_recv()
            group.append(send(ext.at[:, side, pl.ds(place, 128), :], ext.at[:, side, pl.ds(target, 128), :], device))

    base_y, base_x = r * 512 - 128, c * 512 - 128
    low_y = jnp.maximum(base_y, 0) - base_y
    low_x = jnp.maximum(base_x, 0) - base_x
    high_y = jnp.minimum(base_y + 511, rows * 512 - S) - base_y
    high_x = jnp.minimum(base_x + 511, cols * 512 - S) - base_x

    def corner(k):
        return jnp.where(k < 2, low_y, high_y), jnp.where(lax.rem(k, 2) == 0, low_x, high_x)

    def given(k):
        return jnp.clip(off[k, 0] - base_y, 0, 512), jnp.clip(off[k, 1] - base_x, 0, 512)

    def number(k):
        cy, cx = corner(k)
        found = 0
        for n in range(1, 4):
            gy, gx = given(n)
            found = jnp.where((gy == cy) & (gx == cx), n, found)
        return jnp.where(k < 4, found, k)

    for copy in own:
        copy.wait()
    arrived(top)

    @pl.when(r == 0)
    def _():
        arrived(across[2])

    for k in range(2):
        w.gather(k, *corner(jnp.int32(k)))
    run([([], w.v1(0, 0)), (w.s1(0), w.v1(1, 0)), (w.s1(1), w.v2(0)), ([], w.v2(1)), (w.s2(0), w.v1(0, 1)), (w.s2(1), w.v1(1, 1))])

    @pl.when(r != 0)
    def _():
        arrived(across[2])

    arrived(bottom)

    def step(i, carry):
        new, old = lax.rem(i + 1, 4), lax.rem(i + 2, 4)
        following = jnp.minimum(i + 1, 7)
        cy, cx = corner(following)
        gy, gx = given(following)
        w.gather(new, jnp.where(following < 4, cy, gy), jnp.where(following < 4, cx, gx))
        v5 = w.v5(0, old) + w.v5(1, old)
        run([
            (w.vp(number(i - 1)), []),
            (w.s1(0) + w.s1(1), w.v3()),
            (w.s3(0), w.v2(0) + v5[:16]),
            (w.s3(1), w.v2(1) + v5[16:32]),
            (w.s2(0), w.v4(0) + v5[32:48]),
            (w.s2(1), w.v4(1) + v5[48:]),
            (w.s4(0), w.v1(0, new)),
            (w.s4(1), w.v1(1, new)),
        ])

        @pl.when((i >= 2) & (i < 6))
        def _():
            w.deposit(*corner(i - 2))

        @pl.when(i >= 6)
        def _():
            w.keep(i - 6, given(i - 2)[1])
        return carry

    lax.fori_loop(1, 8, step, 0)
    run([(w.vp(7), w.v3()), (w.s3(0), w.v5(0, 2)), (w.s3(1), w.v4(0) + w.v5(1, 2)), (w.s4(0), w.v4(1))])
    w.keep(2, given(6)[1])
    run([(w.s4(1), w.v5(0, 3)), ([], w.v5(1, 3))])

    paired = send(pg.at[1 - core], w.pair, other)
    w.keep(3, given(7)[1])
    places = [(given(k)[0], column(given(k)[1])[0]) for k in range(4, 8)]
    sides = []
    for side in (0, 5):
        w.merge(places, side, 0, 128)
        w.merge(places, side, 640, 128)
        sides.append((send(acc.at[:, side, pl.ds(0, 128), :], w.ybot.at[:, side], up),
                      send(acc.at[:, side, pl.ds(640, 128), :], w.ytop.at[:, side], down)))
    paired.wait_recv()
    for m in range(2):
        w.part[512 * m:512 * m + 512] = pg[core, m] + w.pair[m]
    piece = lambda a, b: pl.ds(pl.multiple_of((a * 4 + b) * PIECE, PIECE), PIECE)
    scattered = [send(w.part.at[piece(*to), :], w.r1.at[n], planes[n]) for n, to in enumerate(plane)]
    middle = []
    for side, into, device in ((0, w.xr, left), (5, w.xl, right)):
        w.merge(places, side, 256, 256)
        middle.append(send(acc.at[:, side, pl.ds(256, 256), :], into.at[:, pl.ds(128, 256), :], device))
    for side in (0, 5):
        w.merge(places, side, 128, 128)
        w.merge(places, side, 512, 128)
    corners = []
    for side, got in zip((0, 5), sides):
        arrived(got)
        for at, came in ((128, w.ytop), (512, w.ybot)):
            for ch in range(2):
                acc[ch, side, at:at + 128] += came[ch, side]
            into, device = (w.xr, left) if side == 0 else (w.xl, right)
            corners.append(send(acc.at[:, side, pl.ds(at, 128), :], into.at[:, pl.ds(at - 128, 128), :], device))
    for j in range(1, 5):
        w.merge(places, j, 0, 128)
        w.merge(places, j, 640, 128)
    along = [send(acc.at[:, pl.ds(1, 4), pl.ds(0, 128), :], w.ybot.at[:, pl.ds(1, 4)], up),
             send(acc.at[:, pl.ds(1, 4), pl.ds(640, 128), :], w.ytop.at[:, pl.ds(1, 4)], down)]
    arrived(scattered)
    total = w.part[piece(y, z), :]
    for n in range(15):
        total = total + w.r1[n]
    w.r2[x] = total
    lined = [send(w.r2.at[x], w.r2.at[x], device) for device in line]
    for j in range(1, 5):
        w.merge(places, j, 128, 512)
    arrived(lined)
    w.full[core, piece(y, z), :] = w.r2[0] + w.r2[1] + w.r2[2] + w.r2[3]
    mine = w.full.at[core, piece(y, z), :]
    spread = [send(mine, mine, device) for device in planes]
    arrived(along)
    for ch in range(2):
        for j in range(1, 5):
            acc[ch, j, 128:256] += w.ytop[ch, j]
            acc[ch, j, 512:640] += w.ybot[ch, j]
    done = [local(acc.at[:, j, pl.ds(128, 512), :], out.at[:, :, pl.ds(128 * (j - 1), 128)]) for j in (2, 3)]
    arrived(middle + corners)
    for ch in range(2):
        acc[ch, 1, 128:640] += w.xl[ch]
        acc[ch, 4, 128:640] += w.xr[ch]
    done += [local(acc.at[:, j, pl.ds(128, 512), :], out.at[:, :, pl.ds(128 * (j - 1), 128)]) for j in (1, 4)]
    arrived(spread)
    last = send(w.full.at[core], w.full.at[core], other)

    def store(h):
        return [local(w.full.at[h, pl.ds((2 * m + k) * S, S), :], probe_out.at[h, m, :, pl.ds(k * H, H)]) for m in range(2) for k in range(2)]

    done += store(core)
    arrived([last])
    done += store(1 - core)
    for copy in done:
        copy.wait()
    send.finish()


def body(object_field, probe, patterns, offsets):
    tables_in = [jnp.asarray(t) for t in tables(S)]
    anywhere = pl.BlockSpec(memory_space=pl.ANY)
    return pl.pallas_call(
        kernel,
        out_shape=(jax.ShapeDtypeStruct(object_field.shape, F32), jax.ShapeDtypeStruct(probe.shape, F32)),
        in_specs=[pl.BlockSpec(memory_space=pltpu.SMEM)] + [anywhere] * 8,
        out_specs=(anywhere, anywhere),
        scratch_shapes=[pltpu.VMEM(*v) for v in SCRATCH.values()] + [
            pltpu.SemaphoreType.DMA((LOCALS,)), pltpu.SemaphoreType.DMA((REMOTES,)), pltpu.SemaphoreType.DMA((REMOTES,))],
        compiler_params=pltpu.CompilerParams(collective_id=0, has_side_effects=True, vmem_limit_bytes=58 * 2**20),
    )(offsets, object_field, probe, patterns, *tables_in)


def solution(mesh):
    in_specs = (P(None, "row", "col"), P(), P(("row", "col"), None, None), P(("row", "col"), None))
    out_specs = (P(None, "row", "col"), P())
    return jax.shard_map(body, mesh=mesh, in_specs=in_specs, out_specs=out_specs, check_vma=False)
```

```python
import functools
import math

import jax
import jax.numpy as jnp
import ml_dtypes
import numpy as np
from jax import lax
from jax.experimental import pallas as pl
from jax.experimental.pallas import tpu as pltpu
from jax.sharding import PartitionSpec as P

BF = jnp.bfloat16
F32 = jnp.float32
H = 128
S = 256
MESH = pl.DeviceIdType.MESH

def split_np(w):
    hi = w.astype(np.float32).astype(ml_dtypes.bfloat16)
    lo = (w - hi.astype(np.float64)).astype(np.float32).astype(ml_dtypes.bfloat16)
    return np.stack([hi, lo])

def tables(n):
    h = n // 2
    a = np.arange(h)
    f = 1.0 / math.sqrt(n)
    out = []
    for par in (0, 1):
        c = np.exp(-2j * np.pi * np.outer(a, 2 * a + par) / n) * f
        fwd = np.block([[c.real, c.imag], [-c.imag, c.real]])
        inv_c = np.conj(c).T
        inv = np.block([[inv_c.real, inv_c.imag], [-inv_c.imag, inv_c.real]])
        out.append((fwd, inv))
    rf = np.stack([split_np(out[p][0]) for p in (0, 1)])
    ri = np.stack([split_np(out[p][1]) for p in (0, 1)])
    cf = np.stack([split_np(out[p][0].T) for p in (0, 1)])
    ci = np.stack([split_np(out[p][1].T) for p in (0, 1)])
    perm = np.zeros((n, n), np.float32)
    for k in range(h):
        perm[2 * k, k] = 1
        perm[2 * k + 1, h + k] = 1
    return rf, cf, ci, ri, perm.astype(ml_dtypes.bfloat16)

def split(x):
    hi = x.astype(BF)
    lo = (x - hi.astype(F32)).astype(BF)
    return hi, lo


def run(steps):
    for mxu, vpu in steps:
        n = max(len(mxu), 1)
        for i in range(n):
            if i < len(mxu):
                mxu[i]()
            for t in vpu[len(vpu) * i // n: len(vpu) * (i + 1) // n]:
                t()

class Work:
    def __init__(self, **refs):
        self.__dict__.update(refs)

    def rows_dot(self, lhs, table, out):
        l = lhs[...]
        t0, t1 = table[0], table[1]
        out[...] = jnp.dot(jnp.concatenate([l, l[:, :S]], axis=1), jnp.concatenate([t0, t0, t1], axis=0), preferred_element_type=F32)

    def cols_dot(self, table, rhs, out):
        r = rhs[...]
        t0, t1 = table[0], table[1]
        out[...] = jnp.dot(jnp.concatenate([t0, t0, t1], axis=1), jnp.concatenate([r, r[:S]], axis=0), preferred_element_type=F32)

    def s1(self, m): return [lambda q=q: self.rows_dot(self.lhs1.at[m, q], self.rf.at[q], self.o1.at[m, q]) for q in range(2)]
    def s2(self, m): return [lambda q=q: self.cols_dot(self.cf.at[q], self.rhs2.at[m, q], self.o2.at[m, q]) for q in range(2)]
    def s3(self): return [lambda q=q: self.cols_dot(self.ci.at[q], self.rhs3a.at[q], self.o3.at[q]) for q in range(2)]
    def s4(self): return [lambda q=q: self.rows_dot(self.lhs4.at[q], self.ri.at[q], self.o4.at[q]) for q in range(2)]
    def s3b(self, p): return [lambda q=q: self.cols_dot(self.ci.at[q], self.rhs3b.at[p, q], self.o3b.at[p % 2, q]) for q in range(2)]
    def s4b(self, p): return [lambda q=q: self.rows_dot(self.lhs4b.at[p % 2, q], self.ri.at[q], self.o4b.at[p % 2, q]) for q in range(2)]

    def put_row(self, ref, rows, re, im):
        hi, lo = split(re)
        ref[rows, 0:H] = hi
        ref[rows, S:S + H] = lo
        hi, lo = split(im)
        ref[rows, H:S] = hi
        ref[rows, S + H:2 * S] = lo

    def put_col(self, ref, row, size, re, im):
        hi, lo = split(re)
        ref[row:row + size] = hi
        ref[S + row:S + row + size] = lo
        hi, lo = split(im)
        ref[H + row:H + row + size] = hi
        ref[S + H + row:S + H + row + size] = lo

    def v1(self, m, slot, size=16):
        def chunk(a):
            rows = slice(a, a + size)
            ar, ai = self.patch[slot, 0, rows], self.patch[slot, 1, rows]
            pr, pi_ = self.probe[0, m, rows], self.probe[1, m, rows]
            er = pr * ar - pi_ * ai
            ei = pr * ai + pi_ * ar
            self.put_row(self.lhs1.at[m, 0], rows, er[:, :H] + er[:, H:], ei[:, :H] + ei[:, H:])
            self.put_row(self.lhs1.at[m, 1], rows, er[:, :H] - er[:, H:], ei[:, :H] - ei[:, H:])
        return [functools.partial(chunk, a) for a in range(0, S, size)]

    def v2(self, m, size=16):
        def chunk(a):
            top, bot = slice(a, a + size), slice(H + a, H + a + size)
            for q in range(2):
                t, b = self.o1[m, q, top], self.o1[m, q, bot]
                p, n = t + b, t - b
                cols = slice(q * H, q * H + H)
                for par, v in ((0, p), (1, n)):
                    self.put_col(self.rhs2.at[m, par, :, cols], a, size, v[:, :H], v[:, H:])
        return [functools.partial(chunk, a) for a in range(0, H, size)]

    def vp(self, number):
        def first():
            hi, lo = split(self.pat[number])
            w = self.perm[...]
            v = jnp.dot(jnp.concatenate([hi, lo], axis=1), jnp.concatenate([w, w], axis=0), preferred_element_type=F32)
            for k in range(2):
                self.pscr[k] = v[:, k * H:(k + 1) * H]
        return [first]

    def v3(self, p, size=16):
        def chunk(q, a):
            re, im = slice(a, a + size), slice(H + a, H + a + size)
            w = [(self.o2[m, q, re], self.o2[m, q, im]) for m in range(2)]
            inten = w[0][0] * w[0][0] + w[0][1] * w[0][1] + w[1][0] * w[1][0] + w[1][1] * w[1][1]
            pat = jnp.concatenate([self.pscr[k, pl.ds(q + 2 * a, size, stride=2), :] for k in range(2)], axis=1)
            mis = 2.0 * (inten - pat)
            for m in range(2):
                self.put_col((self.rhs3b.at[p, q] if m else self.rhs3a.at[q]), a, size, w[m][0] * mis, w[m][1] * mis)
        return [functools.partial(chunk, q, a) for q in range(2) for a in range(0, H, size)]

    def v4(self, size=16):
        return self.halves(self.o3, self.lhs4, size)

    def v4b(self, p, size=16):
        return self.halves(self.o3b.at[p % 2], self.lhs4b.at[p % 2], size)

    def halves(self, o3, lhs4, size):
        def chunk(a):
            for at, op in ((a, lambda x, y: x + y), (H + a, lambda x, y: x - y)):
                re = op(o3[0, a:a + size], o3[1, a:a + size])
                im = op(o3[0, H + a:H + a + size], o3[1, H + a:H + a + size])
                for q in range(2):
                    cols = slice(q * H, q * H + H)
                    self.put_row(lhs4.at[q], slice(at, at + size), re[:, cols], im[:, cols])
        return [functools.partial(chunk, a) for a in range(0, H, size)]

    def v5(self, p, size=8):
        return self.products(0, p, self.o4, size)

    def v5b(self, p, size=8):
        return self.products(1, p, self.o4b.at[p % 2], size)

    def products(self, m, p, o4, size):
        def chunk(a):
            rows = slice(a, a + size)
            A, B = o4[0, rows], o4[1, rows]
            both = (A + B, A - B)
            for k in range(2):
                cols = slice(k * H, k * H + H)
                gr, gi = both[k][:, :H], both[k][:, H:]
                ar, ai = self.patch[p, 0, rows, cols], self.patch[p, 1, rows, cols]
                pr, pi_ = self.probe[0, m, rows, cols], self.probe[1, m, rows, cols]
                at = slice(k * S + a, k * S + a + size)
                self.pg[0, m, at] += ar * gr + ai * gi
                self.pg[1, m, at] += ar * gi - ai * gr
                re = pr * gr + pi_ * gi
                im = pr * gi - pi_ * gr
                if m == 0:
                    self.gsum[p, 0, k, rows] = re
                    self.gsum[p, 1, k, rows] = im
                else:
                    self.gsum[p, 0, k, rows] += re
                    self.gsum[p, 1, k, rows] += im
        return [functools.partial(chunk, a) for a in range(0, S, size)]

    def gather(self, slot, y, x):
        j0 = jnp.minimum(lax.shift_right_logical(x, 7), 3)
        s = x - j0 * 128
        back = (128 - s) & 127
        lane = lax.broadcasted_iota(jnp.int32, (32, 128), 1)
        for c in range(2):
            for a in range(0, S, 32):
                r = [pltpu.roll(self.ext[c, j0 + k, pl.ds(y + a, 32), :], back, 1) for k in range(3)]
                for k in range(2):
                    self.patch[slot, c, a:a + 32, k * 128:(k + 1) * 128] = jnp.where(lane < 128 - s, r[k], r[k + 1])

    def shifted(self, p, a, s):
        lane = lax.broadcasted_iota(jnp.int32, (32, 128), 1)
        for c in range(2):
            g = [pltpu.roll(self.gsum[p, c, k, a:a + 32], s & 127, 1) for k in range(2)]
            yield c, (jnp.where(lane >= s, g[0], 0.0), jnp.where(lane >= s, g[1], g[0]), jnp.where(lane >= s, 0.0, g[1]))

    def deposit(self, p, y, x):
        j0, s = column(x)

        def chunk(a):
            for c, blocks in self.shifted(p, a, s):
                for k in range(3):
                    self.acc[c, j0 + k, pl.ds(y + a, 32), :] += blocks[k]
        return [functools.partial(chunk, a) for a in range(0, S, 32)]

    def keep(self, p, x):
        j0, s = column(x)

        def chunk(a):
            for c, blocks in self.shifted(p, a, s):
                for k in range(3):
                    self.held[p - 4, c, 1 + k, PAD + a:PAD + a + 32] = blocks[k]
        return [functools.partial(chunk, a) for a in range(0, S, 32)]

    def merge(self, places, block, start, size):
        def go(t, carry):
            row = pl.multiple_of(start + t * 32, 32)
            for c in range(2):
                value = self.acc[c, block, pl.ds(row, 32), :]
                for n, (y, j0) in enumerate(places):
                    k = block - j0
                    k = jnp.where((k >= 0) & (k <= 2), k + 1, 0)
                    at = jnp.clip(row - y + PAD, 0, S + PAD)
                    value += self.held[n, c, k, pl.ds(at, 32), :]
                self.acc[c, block, pl.ds(row, 32), :] = value
            return carry
        lax.fori_loop(0, size // 32, go, 0)


PAD = 32


def column(x):
    j0 = jnp.minimum(lax.shift_right_logical(x, 7), 3)
    return j0, x - j0 * 128


def neighbours():
    rows, cols = lax.axis_size("row"), lax.axis_size("col")
    r, c = lax.axis_index("row"), lax.axis_index("col")
    left = (r, lax.rem(c + cols - 1, cols))
    right = (r, lax.rem(c + 1, cols))
    up = (lax.rem(r + rows - 1, rows), c)
    down = (lax.rem(r + 1, rows), c)
    return left, right, up, down


def greet(devices):
    barrier = pltpu.get_barrier_semaphore()
    for device in devices:
        pl.semaphore_signal(barrier, inc=1, device_id=device, device_id_type=MESH)


def met(devices):
    pl.semaphore_wait(pltpu.get_barrier_semaphore(), len(devices))


class Sender:
    def __init__(self, send_sem, recv_sem):
        self.send_sem, self.recv_sem, self.copies = send_sem, recv_sem, []

    def __call__(self, src, dst, device):
        n = len(self.copies)
        copy = pltpu.make_async_remote_copy(
            src_ref=src, dst_ref=dst, send_sem=self.send_sem.at[n], recv_sem=self.recv_sem.at[n],
            device_id=device, device_id_type=MESH)
        copy.start()
        self.copies.append(copy)
        return copy

    def finish(self):
        for copy in self.copies:
            copy.wait_send()


class Local:
    def __init__(self, sem):
        self.sem, self.count = sem, 0

    def __call__(self, src, dst):
        copy = pltpu.make_async_copy(src, dst, self.sem.at[self.count])
        self.count += 1
        copy.start()
        return copy


def arrived(copies):
    for copy in copies:
        copy.wait_recv()


SCRATCH = dict(
    ext=((2, 6, 768, H), F32), acc=((2, 6, 768, H), F32), probe=((2, 2, S, S), F32), pat=((8, S, S), F32),
    rf=((2, 2, S, S), BF), cf=((2, 2, S, S), BF), ci=((2, 2, S, S), BF), ri=((2, 2, S, S), BF), perm=((S, S), BF),
    pg=((2, 2, 512, H), F32), patch=((8, 2, S, S), F32), lhs1=((2, 2, S, 2 * S), BF), o1=((2, 2, S, S), F32), rhs2=((2, 2, 2 * S, S), BF),
    o2=((2, 2, S, S), F32), rhs3a=((2, 2 * S, S), BF), rhs3b=((8, 2, 2 * S, S), BF), o3=((2, S, S), F32), lhs4=((2, S, 2 * S), BF), o4=((2, S, S), F32),
    o3b=((2, 2, S, S), F32), lhs4b=((2, 2, S, 2 * S), BF), o4b=((2, 2, S, S), F32),
    pscr=((2, S, H), F32), gsum=((8, 2, 2, S, H), F32), held=((4, 2, 4, S + 2 * PAD, H), F32),
    ytop=((2, 6, H, H), F32), ybot=((2, 6, H, H), F32), xl=((2, 512, H), F32), xr=((2, 512, H), F32),
    pair=((2, 512, H), F32), part=((2, 512, H), F32), r1=((2, 15, 32, H), F32), r2=((2, 4, 32, H), F32), full=((2, 2, 512, H), F32))
REMOTES = 6 + 2 + 4 + 4 + 2 + 2 + 4 + 2 * 35
LOCALS = 4 + 7 + 4 + 8


def kernel(off, obj, probe_in, pat_in, rf_in, cf_in, ci_in, ri_in, perm_in, out, probe_out, *scr):
    refs = dict(zip(SCRATCH, scr))
    w = Work(**refs)
    ext, acc, pg = w.ext, w.acc, w.pg
    local_sem, send_sem, recv_sem = scr[len(SCRATCH):]
    r, c = lax.axis_index("row"), lax.axis_index("col")
    rows, cols = lax.axis_size("row"), lax.axis_size("col")
    y, core, z, x = lax.div(r, 2), lax.rem(r, 2), lax.div(c, 4), lax.rem(c, 4)
    left, right, up, down = neighbours()
    other = (r + 1 - 2 * core, c)
    turn = lambda i, d: lax.rem(i + d, 4)
    plane = [(turn(y, a), turn(z, b)) for a in range(4) for b in range(4) if a or b]
    planes = [(a * 2 + core, b * 4 + x) for a, b in plane]
    line = [(r, z * 4 + turn(x, d)) for d in (1, 2, 3)]
    everyone = [left, right, up, down, other] + planes + line
    greet(everyone)
    local = Local(local_sem)
    own = [local(obj.at[:, :, pl.ds(128 * j, 128)], ext.at[:, 1 + j, pl.ds(128, 512), :]) for j in range(4)]
    own += [local(a, b) for a, b in ((probe_in, w.probe), (rf_in, w.rf), (cf_in, w.cf), (perm_in, w.perm), (pat_in, w.pat), (ci_in, w.ci), (ri_in, w.ri))]
    for copy in own[:4]:
        copy.wait()
    met(everyone)
    send = Sender(send_sem, recv_sem)

    def side(start, size):
        rows_there = pl.ds(start, size)
        return (send(ext.at[:, 1, rows_there, :], ext.at[:, 5, rows_there, :], left),
                send(ext.at[:, 4, rows_there, :], ext.at[:, 0, rows_there, :], right))

    inner = pl.ds(1, 4)
    across = [side(504, 136)]
    top = [send(ext.at[:, inner, pl.ds(512, 128), :], ext.at[:, inner, pl.ds(0, 128), :], down)]
    across.append(side(128, 128))
    bottom = [send(ext.at[:, inner, pl.ds(128, 128), :], ext.at[:, inner, pl.ds(640, 128), :], up)]
    across.append(side(256, 248))
    acc[...] = jnp.zeros_like(acc)
    pg[...] = jnp.zeros_like(pg)
    w.held[:, :, 0] = jnp.zeros((4, 2, S + 2 * PAD, H), F32)
    w.held[:, :, 1:4, 0:PAD] = jnp.zeros((4, 2, 3, PAD, H), F32)
    w.held[:, :, 1:4, S + PAD:] = jnp.zeros((4, 2, 3, PAD, H), F32)

    for k, (place, target, device, group) in enumerate(((512, 0, down, top), (128, 640, up, bottom))):
        for block, copy in zip((5, 0), across[k]):
            copy.wait_recv()
            group.append(send(ext.at[:, block, pl.ds(place, 128), :], ext.at[:, block, pl.ds(target, 128), :], device))

    base_y, base_x = r * 512 - 128, c * 512 - 128
    low_y = jnp.maximum(base_y, 0) - base_y
    low_x = jnp.maximum(base_x, 0) - base_x
    high_y = jnp.minimum(base_y + 511, rows * 512 - S) - base_y
    high_x = jnp.minimum(base_x + 511, cols * 512 - S) - base_x

    def corner(k):
        return jnp.where(k < 2, low_y, high_y), jnp.where(lax.rem(k, 2) == 0, low_x, high_x)

    def given(k):
        return jnp.clip(off[k, 0] - base_y, 0, 512), jnp.clip(off[k, 1] - base_x, 0, 512)

    def number(k):
        cy, cx = corner(k)
        found = 0
        for n in range(1, 4):
            gy, gx = given(n)
            found = jnp.where((gy == cy) & (gx == cx), n, found)
        return jnp.where(k < 4, found, k)

    for copy in own[4:]:
        copy.wait()
    arrived(top)

    @pl.when(r == 0)
    def _():
        arrived(across[2])

    for k in range(2):
        w.gather(k, *corner(jnp.int32(k)))
    run([([], w.v1(0, 0)), (w.s1(0), w.v1(1, 0)), (w.s1(1), w.v2(0)), ([], w.v2(1)), (w.s2(0), w.v1(0, 1)), (w.s2(1), w.v1(1, 1))])

    piece = lambda a, b: pl.ds(pl.multiple_of((a * 4 + b) * 32, 32), 32)

    def chain(m):
        copies = [send(pg.at[1 - core, m], w.pair.at[m], other)]
        yield
        arrived(copies)
        w.part[m] = pg[core, m] + w.pair[m]
        copies = [send(w.part.at[m, piece(*to), :], w.r1.at[m, n], planes[n]) for n, to in enumerate(plane)]
        yield
        arrived(copies)
        total = w.part[m, piece(y, z), :]
        for n in range(15):
            total = total + w.r1[m, n]
        w.r2[m, x] = total
        mine = w.r2.at[m, x]
        copies = [send(mine, mine, device) for device in line]
        yield
        arrived(copies)
        w.full[core, m, piece(y, z), :] = w.r2[m, 0] + w.r2[m, 1] + w.r2[m, 2] + w.r2[m, 3]
        mine = w.full.at[core, m, piece(y, z), :]
        copies = [send(mine, mine, device) for device in planes]
        yield
        arrived(copies)
        mine = w.full.at[core, m]
        copies = [send(mine, mine, other)]
        yield
        arrived(copies)
        yield

    chains = [chain(0), chain(1)]

    run([
        (w.vp(number(jnp.int32(0))), []),
        (w.s1(0) + w.s1(1), w.v3(0)),
        (w.s3(), w.v2(0) + w.v2(1)),
        (w.s2(0), w.v4()),
        (w.s2(1), []),
    ])

    @pl.when(r != 0)
    def _():
        arrived(across[2])

    arrived(bottom)

    w.gather(2, *corner(jnp.int32(2)))
    run([(w.s4(), w.v1(0, 2) + w.v1(1, 2))])

    def step(i, carry):
        new, old = jnp.minimum(i + 1, 7), i - 2
        cy, cx = corner(new)
        gy, gx = given(new)
        w.gather(new, jnp.where(new < 4, cy, gy), jnp.where(new < 4, cx, gx))
        v5 = w.v5(old)
        run([
            (w.vp(number(i - 1)), []),
            (w.s1(0) + w.s1(1), w.v3(i - 1) + v5[:12]),
            (w.s3(), w.v2(0) + w.v2(1)),
            (w.s2(0), w.v4() + v5[12:26]),
            (w.s2(1), v5[26:] + w.v1(0, new)),
            (w.s4(), w.v1(1, new)),
        ])
        return carry

    lax.fori_loop(2, 8, step, 0)

    def settled(p):
        return w.deposit(p, *corner(jnp.int32(p))) if p < 4 else w.keep(p, given(p)[1])

    run([(w.vp(7), []), ([], w.v3(7)), (w.s3(), w.v5(6)), (w.s3b(0), w.v4()), (w.s4(), w.v4b(0)), (w.s3b(1), w.v5(7))])
    next(chains[0])
    run([(w.s4b(0), w.v4b(1)), (w.s3b(2), w.v5b(0) + settled(0)), (w.s4b(1), w.v4b(2))])
    next(chains[0])
    for p in range(3, 8):
        run([(w.s3b(p), w.v5b(p - 2) + settled(p - 2)), (w.s4b(p - 1), w.v4b(p))])
    run([(w.s4b(7), w.v5b(6))])
    run([([], w.v5b(7))])
    next(chains[1])
    next(chains[0])
    run([([], settled(6) + settled(7))])
    next(chains[1])
    places = [(given(k)[0], column(given(k)[1])[0]) for k in range(4, 8)]
    sides = []
    for block in (0, 5):
        w.merge(places, block, 0, 128)
        w.merge(places, block, 640, 128)
        sides.append((send(acc.at[:, block, pl.ds(0, 128), :], w.ybot.at[:, block], up),
                      send(acc.at[:, block, pl.ds(640, 128), :], w.ytop.at[:, block], down)))
    middle = []
    for block, into, device in ((0, w.xr, left), (5, w.xl, right)):
        w.merge(places, block, 256, 256)
        middle.append(send(acc.at[:, block, pl.ds(256, 256), :], into.at[:, pl.ds(128, 256), :], device))
    for j in range(1, 5):
        w.merge(places, j, 0, 128)
        w.merge(places, j, 640, 128)
    along = [send(acc.at[:, inner, pl.ds(0, 128), :], w.ybot.at[:, inner], up),
             send(acc.at[:, inner, pl.ds(640, 128), :], w.ytop.at[:, inner], down)]
    for block in (0, 5):
        w.merge(places, block, 128, 128)
        w.merge(places, block, 512, 128)
    corners = []
    for block, got in zip((0, 5), sides):
        arrived(got)
        for row, came in ((128, w.ytop), (512, w.ybot)):
            for ch in range(2):
                acc[ch, block, row:row + 128] += came[ch, block]
            into, device = (w.xr, left) if block == 0 else (w.xl, right)
            corners.append(send(acc.at[:, block, pl.ds(row, 128), :], into.at[:, pl.ds(row - 128, 128), :], device))
    next(chains[0])
    for j in range(1, 5):
        w.merge(places, j, 128, 512)
    next(chains[1])
    next(chains[0])
    arrived(along)
    for ch in range(2):
        for j in range(1, 5):
            acc[ch, j, 128:256] += w.ytop[ch, j]
            acc[ch, j, 512:640] += w.ybot[ch, j]
    done = [local(acc.at[:, j, pl.ds(128, 512), :], out.at[:, :, pl.ds(128 * (j - 1), 128)]) for j in (2, 3)]

    def store(h, m):
        return [local(w.full.at[h, m, pl.ds(k * S, S), :], probe_out.at[h, m, :, pl.ds(k * H, H)]) for k in range(2)]

    done += store(core, 0)
    next(chains[1])
    arrived(middle + corners)
    for ch in range(2):
        acc[ch, 1, 128:640] += w.xl[ch]
        acc[ch, 4, 128:640] += w.xr[ch]
    done += [local(acc.at[:, j, pl.ds(128, 512), :], out.at[:, :, pl.ds(128 * (j - 1), 128)]) for j in (1, 4)]
    next(chains[0])
    done += store(1 - core, 0)
    next(chains[1])
    done += store(core, 1)
    next(chains[1])
    done += store(1 - core, 1)
    for copy in done:
        copy.wait()
    send.finish()


def place_kernel(a, b, out_a, out_b, held_a, held_b, sem):
    parts = [((n // 4, pl.ds(128 * (n % 4), 128)), a, held_a, out_a) for n in range(8)]
    parts += [((n // 2, n % 2), b, held_b, out_b) for n in range(4)]
    first = [pltpu.make_async_copy(src.at[at], held.at[at], sem.at[0, n]) for n, (at, src, held, dst) in enumerate(parts)]
    second = [pltpu.make_async_copy(held.at[at], dst.at[at], sem.at[1, n]) for n, (at, src, held, dst) in enumerate(parts)]
    for copy in first:
        copy.start()
    for one, two in zip(first, second):
        one.wait()
        two.start()
    for copy in second:
        copy.wait()


def placed(a, b):
    anywhere = pl.BlockSpec(memory_space=pl.ANY)
    return pl.pallas_call(
        place_kernel,
        out_shape=(jax.ShapeDtypeStruct(a.shape, F32), jax.ShapeDtypeStruct(b.shape, F32)),
        in_specs=[anywhere] * 2,
        out_specs=(anywhere, anywhere),
        scratch_shapes=[pltpu.VMEM(a.shape, F32), pltpu.VMEM(b.shape, F32), pltpu.SemaphoreType.DMA((2, 12))],
        compiler_params=pltpu.CompilerParams(vmem_limit_bytes=60 * 2**20),
    )(a, b)


def body(object_field, probe, patterns, offsets):
    tables_in = [jnp.asarray(t) for t in tables(S)]
    anywhere = pl.BlockSpec(memory_space=pl.ANY)
    return placed(*pl.pallas_call(
        kernel,
        out_shape=(jax.ShapeDtypeStruct(object_field.shape, F32), jax.ShapeDtypeStruct(probe.shape, F32)),
        in_specs=[pl.BlockSpec(memory_space=pltpu.SMEM)] + [anywhere] * 8,
        out_specs=(anywhere, anywhere),
        scratch_shapes=[pltpu.VMEM(*v) for v in SCRATCH.values()] + [
            pltpu.SemaphoreType.DMA((LOCALS,)), pltpu.SemaphoreType.DMA((REMOTES,)), pltpu.SemaphoreType.DMA((REMOTES,))],
        compiler_params=pltpu.CompilerParams(collective_id=0, has_side_effects=True, vmem_limit_bytes=58 * 2**20),
    )(offsets, object_field, probe, patterns, *tables_in))


def solution(mesh):
    in_specs = (P(None, "row", "col"), P(), P(("row", "col"), None, None), P(("row", "col"), None))
    out_specs = (P(None, "row", "col"), P())
    return jax.shard_map(body, mesh=mesh, in_specs=in_specs, out_specs=out_specs, check_vma=False)
```

```python
import functools
import math

import jax
import jax.numpy as jnp
import ml_dtypes
import numpy as np
from jax import lax
from jax.experimental import pallas as pl
from jax.experimental.pallas import tpu as pltpu
from jax.sharding import PartitionSpec as P

BF = jnp.bfloat16
F32 = jnp.float32
H = 128
S = 256
MESH = pl.DeviceIdType.MESH

def split_np(w):
    hi = w.astype(np.float32).astype(ml_dtypes.bfloat16)
    lo = (w - hi.astype(np.float64)).astype(np.float32).astype(ml_dtypes.bfloat16)
    return np.stack([hi, lo])

def tables(n):
    h = n // 2
    a = np.arange(h)
    f = 1.0 / math.sqrt(n)
    out = []
    for par in (0, 1):
        c = np.exp(-2j * np.pi * np.outer(a, 2 * a + par) / n) * f
        fwd = np.block([[c.real, c.imag], [-c.imag, c.real]])
        inv_c = np.conj(c).T
        inv = np.block([[inv_c.real, inv_c.imag], [-inv_c.imag, inv_c.real]])
        out.append((fwd, inv))
    rf = np.stack([split_np(out[p][0]) for p in (0, 1)])
    ri = np.stack([split_np(out[p][1]) for p in (0, 1)])
    cf = np.stack([split_np(out[p][0].T) for p in (0, 1)])
    ci = np.stack([split_np(out[p][1].T) for p in (0, 1)])
    perm = np.zeros((n, n), np.float32)
    for k in range(h):
        perm[2 * k, k] = 1
        perm[2 * k + 1, h + k] = 1
    return rf, cf, ci, ri, perm.astype(ml_dtypes.bfloat16)

def split(x):
    hi = x.astype(BF)
    lo = (x - hi.astype(F32)).astype(BF)
    return hi, lo


def run(steps):
    for mxu, vpu in steps:
        n = max(len(mxu), 1)
        for i in range(n):
            if i < len(mxu):
                mxu[i]()
            for t in vpu[len(vpu) * i // n: len(vpu) * (i + 1) // n]:
                t()

class Work:
    def __init__(self, **refs):
        self.__dict__.update(refs)

    def rows_dot(self, lhs, table, out):
        l = lhs[...]
        t0, t1 = table[0], table[1]
        out[...] = jnp.dot(jnp.concatenate([l, l[:, :S]], axis=1), jnp.concatenate([t0, t0, t1], axis=0), preferred_element_type=F32)

    def cols_dot(self, table, rhs, out):
        r = rhs[...]
        t0, t1 = table[0], table[1]
        out[...] = jnp.dot(jnp.concatenate([t0, t0, t1], axis=1), jnp.concatenate([r, r[:S]], axis=0), preferred_element_type=F32)

    def s1(self, m): return [lambda q=q: self.rows_dot(self.lhs1.at[m, q], self.rf.at[q], self.o1.at[m, q]) for q in range(2)]
    def s2(self, m): return [lambda q=q: self.cols_dot(self.cf.at[q], self.rhs2.at[m, q], self.o2.at[m, q]) for q in range(2)]
    def s3(self): return [lambda q=q: self.cols_dot(self.ci.at[q], self.rhs3a.at[q], self.o3.at[q]) for q in range(2)]
    def s4(self): return [lambda q=q: self.rows_dot(self.lhs4.at[q], self.ri.at[q], self.o4.at[q]) for q in range(2)]
    def s3b(self, p): return [lambda q=q: self.cols_dot(self.ci.at[q], self.rhs3b.at[p, q], self.o3b.at[p % 2, q]) for q in range(2)]
    def s4b(self, p): return [lambda q=q: self.rows_dot(self.lhs4b.at[p % 2, q], self.ri.at[q], self.o4b.at[p % 2, q]) for q in range(2)]

    def put_row(self, ref, rows, re, im):
        hi, lo = split(re)
        ref[rows, 0:H] = hi
        ref[rows, S:S + H] = lo
        hi, lo = split(im)
        ref[rows, H:S] = hi
        ref[rows, S + H:2 * S] = lo

    def put_col(self, ref, row, size, re, im):
        hi, lo = split(re)
        ref[row:row + size] = hi
        ref[S + row:S + row + size] = lo
        hi, lo = split(im)
        ref[H + row:H + row + size] = hi
        ref[S + H + row:S + H + row + size] = lo

    def v1(self, m, slot, size=16):
        def chunk(a):
            rows = slice(a, a + size)
            ar, ai = self.patch[slot, 0, rows], self.patch[slot, 1, rows]
            pr, pi_ = self.probe[0, m, rows], self.probe[1, m, rows]
            er = pr * ar - pi_ * ai
            ei = pr * ai + pi_ * ar
            self.put_row(self.lhs1.at[m, 0], rows, er[:, :H] + er[:, H:], ei[:, :H] + ei[:, H:])
            self.put_row(self.lhs1.at[m, 1], rows, er[:, :H] - er[:, H:], ei[:, :H] - ei[:, H:])
        return [functools.partial(chunk, a) for a in range(0, S, size)]

    def v2(self, m, size=16):
        def chunk(a):
            top, bot = slice(a, a + size), slice(H + a, H + a + size)
            for q in range(2):
                t, b = self.o1[m, q, top], self.o1[m, q, bot]
                p, n = t + b, t - b
                cols = slice(q * H, q * H + H)
                for par, v in ((0, p), (1, n)):
                    self.put_col(self.rhs2.at[m, par, :, cols], a, size, v[:, :H], v[:, H:])
        return [functools.partial(chunk, a) for a in range(0, H, size)]

    def vp(self, number):
        def first():
            hi, lo = split(self.pat[number])
            w = self.perm[...]
            v = jnp.dot(jnp.concatenate([hi, lo], axis=1), jnp.concatenate([w, w], axis=0), preferred_element_type=F32)
            for k in range(2):
                self.pscr[k] = v[:, k * H:(k + 1) * H]
        return [first]

    def v3(self, p, size=16):
        def chunk(q, a):
            re, im = slice(a, a + size), slice(H + a, H + a + size)
            w = [(self.o2[m, q, re], self.o2[m, q, im]) for m in range(2)]
            inten = w[0][0] * w[0][0] + w[0][1] * w[0][1] + w[1][0] * w[1][0] + w[1][1] * w[1][1]
            pat = jnp.concatenate([self.pscr[k, pl.ds(q + 2 * a, size, stride=2), :] for k in range(2)], axis=1)
            mis = 2.0 * (inten - pat)
            for m in range(2):
                self.put_col((self.rhs3b.at[p, q] if m else self.rhs3a.at[q]), a, size, w[m][0] * mis, w[m][1] * mis)
        return [functools.partial(chunk, q, a) for q in range(2) for a in range(0, H, size)]

    def v4(self, size=16):
        return self.halves(self.o3, self.lhs4, size)

    def v4b(self, p, size=16):
        return self.halves(self.o3b.at[p % 2], self.lhs4b.at[p % 2], size)

    def halves(self, o3, lhs4, size):
        def chunk(a):
            for at, op in ((a, lambda x, y: x + y), (H + a, lambda x, y: x - y)):
                re = op(o3[0, a:a + size], o3[1, a:a + size])
                im = op(o3[0, H + a:H + a + size], o3[1, H + a:H + a + size])
                for q in range(2):
                    cols = slice(q * H, q * H + H)
                    self.put_row(lhs4.at[q], slice(at, at + size), re[:, cols], im[:, cols])
        return [functools.partial(chunk, a) for a in range(0, H, size)]

    def v5(self, p, size=8):
        return self.products(0, p, self.o4, size)

    def v5b(self, p, size=8):
        return self.products(1, p, self.o4b.at[p % 2], size)

    def products(self, m, p, o4, size):
        def chunk(a):
            rows = slice(a, a + size)
            A, B = o4[0, rows], o4[1, rows]
            both = (A + B, A - B)
            for k in range(2):
                cols = slice(k * H, k * H + H)
                gr, gi = both[k][:, :H], both[k][:, H:]
                ar, ai = self.patch[p, 0, rows, cols], self.patch[p, 1, rows, cols]
                pr, pi_ = self.probe[0, m, rows, cols], self.probe[1, m, rows, cols]
                at = slice(k * S + a, k * S + a + size)
                self.pg[0, m, at] += ar * gr + ai * gi
                self.pg[1, m, at] += ar * gi - ai * gr
                re = pr * gr + pi_ * gi
                im = pr * gi - pi_ * gr
                if m == 0:
                    self.gsum[p, 0, k, rows] = re
                    self.gsum[p, 1, k, rows] = im
                else:
                    self.gsum[p, 0, k, rows] += re
                    self.gsum[p, 1, k, rows] += im
        return [functools.partial(chunk, a) for a in range(0, S, size)]

    def gather(self, slot, y, x):
        j0 = jnp.minimum(lax.shift_right_logical(x, 7), 3)
        s = x - j0 * 128
        back = (128 - s) & 127
        lane = lax.broadcasted_iota(jnp.int32, (32, 128), 1)
        for c in range(2):
            for a in range(0, S, 32):
                r = [pltpu.roll(self.ext[c, j0 + k, pl.ds(y + a, 32), :], back, 1) for k in range(3)]
                for k in range(2):
                    self.patch[slot, c, a:a + 32, k * 128:(k + 1) * 128] = jnp.where(lane < 128 - s, r[k], r[k + 1])

    def shifted(self, p, a, s):
        lane = lax.broadcasted_iota(jnp.int32, (32, 128), 1)
        for c in range(2):
            g = [pltpu.roll(self.gsum[p, c, k, a:a + 32], s & 127, 1) for k in range(2)]
            yield c, (jnp.where(lane >= s, g[0], 0.0), jnp.where(lane >= s, g[1], g[0]), jnp.where(lane >= s, 0.0, g[1]))

    def deposit(self, p, y, x):
        j0, s = column(x)

        def chunk(a):
            for c, blocks in self.shifted(p, a, s):
                for k in range(3):
                    self.acc[c, j0 + k, pl.ds(y + a, 32), :] += blocks[k]
        return [functools.partial(chunk, a) for a in range(0, S, 32)]

    def keep(self, p, x):
        j0, s = column(x)

        def chunk(a):
            for c, blocks in self.shifted(p, a, s):
                for k in range(3):
                    self.held[p - 4, c, 1 + k, PAD + a:PAD + a + 32] = blocks[k]
        return [functools.partial(chunk, a) for a in range(0, S, 32)]

    def merge(self, places, block, start, size):
        def go(t, carry):
            row = pl.multiple_of(start + t * 32, 32)
            for c in range(2):
                value = self.acc[c, block, pl.ds(row, 32), :]
                for n, (y, j0) in enumerate(places):
                    k = block - j0
                    k = jnp.where((k >= 0) & (k <= 2), k + 1, 0)
                    at = jnp.clip(row - y + PAD, 0, S + PAD)
                    value += self.held[n, c, k, pl.ds(at, 32), :]
                self.acc[c, block, pl.ds(row, 32), :] = value
            return carry
        lax.fori_loop(0, size // 32, go, 0)


PAD = 32


def column(x):
    j0 = jnp.minimum(lax.shift_right_logical(x, 7), 3)
    return j0, x - j0 * 128


def neighbours():
    rows, cols = lax.axis_size("row"), lax.axis_size("col")
    r, c = lax.axis_index("row"), lax.axis_index("col")
    left = (r, lax.rem(c + cols - 1, cols))
    right = (r, lax.rem(c + 1, cols))
    up = (lax.rem(r + rows - 1, rows), c)
    down = (lax.rem(r + 1, rows), c)
    return left, right, up, down


def greet(devices):
    barrier = pltpu.get_barrier_semaphore()
    for device in devices:
        pl.semaphore_signal(barrier, inc=1, device_id=device, device_id_type=MESH)


def met(devices):
    pl.semaphore_wait(pltpu.get_barrier_semaphore(), len(devices))


class Sender:
    def __init__(self, send_sem, recv_sem):
        self.send_sem, self.recv_sem, self.copies = send_sem, recv_sem, []

    def __call__(self, src, dst, device, start=True):
        n = len(self.copies)
        copy = pltpu.make_async_remote_copy(
            src_ref=src, dst_ref=dst, send_sem=self.send_sem.at[n], recv_sem=self.recv_sem.at[n],
            device_id=device, device_id_type=MESH)
        if start:
            copy.start()
        self.copies.append(copy)
        return copy

    def finish(self):
        for copy in self.copies:
            copy.wait_send()


class Local:
    def __init__(self, sem):
        self.sem, self.count = sem, 0

    def __call__(self, src, dst):
        copy = pltpu.make_async_copy(src, dst, self.sem.at[self.count])
        self.count += 1
        copy.start()
        return copy


def arrived(copies):
    for copy in copies:
        copy.wait_recv()


SCRATCH = dict(
    ext=((2, 6, 768, H), F32), acc=((2, 6, 768, H), F32), probe=((2, 2, S, S), F32), pat=((8, S, S), F32),
    rf=((2, 2, S, S), BF), cf=((2, 2, S, S), BF), ci=((2, 2, S, S), BF), ri=((2, 2, S, S), BF), perm=((S, S), BF),
    pg=((2, 2, 512, H), F32), patch=((8, 2, S, S), F32), lhs1=((2, 2, S, 2 * S), BF), o1=((2, 2, S, S), F32), rhs2=((2, 2, 2 * S, S), BF),
    o2=((2, 2, S, S), F32), rhs3a=((2, 2 * S, S), BF), rhs3b=((8, 2, 2 * S, S), BF), o3=((2, S, S), F32), lhs4=((2, S, 2 * S), BF), o4=((2, S, S), F32),
    o3b=((2, 2, S, S), F32), lhs4b=((2, 2, S, 2 * S), BF), o4b=((2, 2, S, S), F32),
    pscr=((2, S, H), F32), gsum=((8, 2, 2, S, H), F32), held=((4, 2, 4, S + 2 * PAD, H), F32),
    ytop=((2, 6, H, H), F32), ybot=((2, 6, H, H), F32), xl=((2, 512, H), F32), xr=((2, 512, H), F32),
    pair=((2, 512, H), F32), part=((2, 512, H), F32), r1=((2, 15, 32, H), F32), r2=((2, 4, 32, H), F32), full=((2, 2, 512, H), F32))
REMOTES = 6 + 2 + 4 + 4 + 2 + 2 + 4 + 2 * 35
LOCALS = 4 + 7 + 4 + 8


def kernel(off, obj, probe_in, pat_in, rf_in, cf_in, ci_in, ri_in, perm_in, out, probe_out, *scr):
    refs = dict(zip(SCRATCH, scr))
    w = Work(**refs)
    ext, acc, pg = w.ext, w.acc, w.pg
    local_sem, send_sem, recv_sem = scr[len(SCRATCH):]
    r, c = lax.axis_index("row"), lax.axis_index("col")
    rows, cols = lax.axis_size("row"), lax.axis_size("col")
    y, core, z, x = lax.div(r, 2), lax.rem(r, 2), lax.div(c, 4), lax.rem(c, 4)
    left, right, up, down = neighbours()
    other = (r + 1 - 2 * core, c)
    turn = lambda i, d: lax.rem(i + d, 4)
    plane = [(turn(y, a), turn(z, b)) for a in range(4) for b in range(4) if a or b]
    planes = [(a * 2 + core, b * 4 + x) for a, b in plane]
    line = [(r, z * 4 + turn(x, d)) for d in (1, 2, 3)]
    everyone = [left, right, up, down, other] + planes + line
    greet(everyone)
    local = Local(local_sem)
    own = [local(obj.at[:, :, pl.ds(128 * j, 128)], ext.at[:, 1 + j, pl.ds(128, 512), :]) for j in range(4)]
    own += [local(a, b) for a, b in ((probe_in, w.probe), (rf_in, w.rf), (cf_in, w.cf), (perm_in, w.perm), (pat_in, w.pat), (ci_in, w.ci), (ri_in, w.ri))]
    for copy in own[:4]:
        copy.wait()
    met(everyone)
    send = Sender(send_sem, recv_sem)

    def side(start, size):
        rows_there = pl.ds(start, size)
        return (send(ext.at[:, 1, rows_there, :], ext.at[:, 5, rows_there, :], left),
                send(ext.at[:, 4, rows_there, :], ext.at[:, 0, rows_there, :], right))

    inner = pl.ds(1, 4)
    across = [side(504, 136)]
    top = [send(ext.at[:, inner, pl.ds(512, 128), :], ext.at[:, inner, pl.ds(0, 128), :], down)]
    across.append(side(128, 128))
    bottom = [send(ext.at[:, inner, pl.ds(128, 128), :], ext.at[:, inner, pl.ds(640, 128), :], up)]
    across.append(side(256, 248))
    acc[...] = jnp.zeros_like(acc)
    pg[...] = jnp.zeros_like(pg)
    w.held[:, :, 0] = jnp.zeros((4, 2, S + 2 * PAD, H), F32)
    w.held[:, :, 1:4, 0:PAD] = jnp.zeros((4, 2, 3, PAD, H), F32)
    w.held[:, :, 1:4, S + PAD:] = jnp.zeros((4, 2, 3, PAD, H), F32)

    for k, (place, target, device, group) in enumerate(((512, 0, down, top), (128, 640, up, bottom))):
        for block, copy in zip((5, 0), across[k]):
            copy.wait_recv()
            group.append(send(ext.at[:, block, pl.ds(place, 128), :], ext.at[:, block, pl.ds(target, 128), :], device))

    base_y, base_x = r * 512 - 128, c * 512 - 128
    low_y = jnp.maximum(base_y, 0) - base_y
    low_x = jnp.maximum(base_x, 0) - base_x
    high_y = jnp.minimum(base_y + 511, rows * 512 - S) - base_y
    high_x = jnp.minimum(base_x + 511, cols * 512 - S) - base_x

    def corner(k):
        return jnp.where(k < 2, low_y, high_y), jnp.where(lax.rem(k, 2) == 0, low_x, high_x)

    def given(k):
        return jnp.clip(off[k, 0] - base_y, 0, 512), jnp.clip(off[k, 1] - base_x, 0, 512)

    def number(k):
        cy, cx = corner(k)
        found = 0
        for n in range(1, 4):
            gy, gx = given(n)
            found = jnp.where((gy == cy) & (gx == cx), n, found)
        return jnp.where(k < 4, found, k)

    for copy in own[4:]:
        copy.wait()
    arrived(top)

    @pl.when(r == 0)
    def _():
        arrived(across[2])

    for k in range(2):
        w.gather(k, *corner(jnp.int32(k)))
    run([([], w.v1(0, 0)), (w.s1(0), w.v1(1, 0)), (w.s1(1), w.v2(0)), ([], w.v2(1)), (w.s2(0), w.v1(0, 1)), (w.s2(1), w.v1(1, 1))])

    piece = lambda a, b: pl.ds(pl.multiple_of((a * 4 + b) * 32, 32), 32)

    def chain(m):
        copies = [send(pg.at[1 - core, m], w.pair.at[m], other)]
        yield
        arrived(copies)
        w.part[m] = pg[core, m] + w.pair[m]
        copies = [send(w.part.at[m, piece(*to), :], w.r1.at[m, n], planes[n]) for n, to in enumerate(plane)]
        yield
        arrived(copies)
        total = w.part[m, piece(y, z), :]
        for n in range(15):
            total = total + w.r1[m, n]
        w.r2[m, x] = total
        mine = w.r2.at[m, x]
        copies = [send(mine, mine, device) for device in line]
        yield
        arrived(copies)
        w.full[core, m, piece(y, z), :] = w.r2[m, 0] + w.r2[m, 1] + w.r2[m, 2] + w.r2[m, 3]
        mine = w.full.at[core, m, piece(y, z), :]
        copies = [send(mine, mine, device) for device in planes]
        yield
        arrived(copies)
        mine = w.full.at[core, m]
        copies = [send(mine, mine, other)]
        yield
        arrived(copies)
        yield

    chains = [chain(0), chain(1)]

    run([
        (w.vp(number(jnp.int32(0))), []),
        (w.s1(0) + w.s1(1), w.v3(0)),
        (w.s3(), w.v2(0) + w.v2(1)),
        (w.s2(0), w.v4()),
        (w.s2(1), []),
    ])

    @pl.when(r != 0)
    def _():
        arrived(across[2])

    arrived(bottom)

    w.gather(2, *corner(jnp.int32(2)))
    run([(w.s4(), w.v1(0, 2) + w.v1(1, 2))])

    def step(i, carry):
        new, old = jnp.minimum(i + 1, 7), i - 2
        cy, cx = corner(new)
        gy, gx = given(new)
        w.gather(new, jnp.where(new < 4, cy, gy), jnp.where(new < 4, cx, gx))
        v5 = w.v5(old)
        run([
            (w.vp(number(i - 1)), []),
            (w.s1(0) + w.s1(1), w.v3(i - 1) + v5[:12]),
            (w.s3(), w.v2(0) + w.v2(1)),
            (w.s2(0), w.v4() + v5[12:26]),
            (w.s2(1), v5[26:] + w.v1(0, new)),
            (w.s4(), w.v1(1, new)),
        ])
        return carry

    lax.fori_loop(2, 8, step, 0)

    def settled(p):
        return w.deposit(p, *corner(jnp.int32(p))) if p < 4 else w.keep(p, given(p)[1])

    turned = [4, 5, 6, 7, 0, 1, 2, 3]
    run([(w.vp(7), []), ([], w.v3(7)), (w.s3(), w.v5(6)), (w.s3b(4), w.v4()), (w.s4(), w.v4b(4)), (w.s3b(5), w.v5(7))])
    next(chains[0])
    run([(w.s4b(4), w.v4b(5)), (w.s3b(6), w.v5b(4) + settled(4)), (w.s4b(5), w.v4b(6))])
    next(chains[0])
    places = [(given(k)[0], column(given(k)[1])[0]) for k in range(4, 8)]
    outer = (r == 0) | (r == rows - 1)
    middle = []
    for n in range(3, 8):
        old = turned[n - 2]
        run([(w.s3b(turned[n]), w.v5b(old) + settled(old)), (w.s4b(turned[n - 1]), w.v4b(turned[n]))])
        if n == 5:
            for block, into, device in ((0, w.xr, left), (5, w.xl, right)):
                w.merge(places, block, 256, 256)
                middle.append(send(acc.at[:, block, pl.ds(256, 248), :], into.at[:, pl.ds(128, 248), :], device, start=False))

            @pl.when(jnp.logical_not(outer))
            def _():
                for copy in middle:
                    copy.start()

            for block in (0, 5):
                w.merge(places, block, 0, 128)
                w.merge(places, block, 640, 128)
    run([(w.s4b(3), w.v5b(2) + settled(2))])
    run([([], w.v5b(3))])
    next(chains[1])
    next(chains[0])
    run([([], settled(3))])
    next(chains[1])

    @pl.when(outer)
    def _():
        for copy in middle:
            copy.start()

    sides = []
    for block in (0, 5):
        sides.append((send(acc.at[:, block, pl.ds(0, 128), :], w.ybot.at[:, block], up),
                      send(acc.at[:, block, pl.ds(640, 128), :], w.ytop.at[:, block], down)))
    for j in range(1, 5):
        w.merge(places, j, 0, 128)
        w.merge(places, j, 640, 128)
    along = [send(acc.at[:, inner, pl.ds(0, 128), :], w.ybot.at[:, inner], up),
             send(acc.at[:, inner, pl.ds(640, 128), :], w.ytop.at[:, inner], down)]
    for block in (0, 5):
        w.merge(places, block, 128, 128)
        w.merge(places, block, 512, 128)
    corners = []
    for block, got in zip((0, 5), sides):
        arrived(got)
        for row, came, start, size in ((128, w.ytop, 128, 128), (512, w.ybot, 504, 136)):
            for ch in range(2):
                acc[ch, block, row:row + 128] += came[ch, block]
            into, device = (w.xr, left) if block == 0 else (w.xl, right)
            corners.append(send(acc.at[:, block, pl.ds(start, size), :], into.at[:, pl.ds(start - 128, size), :], device))
    next(chains[0])
    for j in range(1, 5):
        w.merge(places, j, 128, 512)
    next(chains[1])
    next(chains[0])
    arrived(along)
    for ch in range(2):
        for j in range(1, 5):
            acc[ch, j, 128:256] += w.ytop[ch, j]
            acc[ch, j, 512:640] += w.ybot[ch, j]
    done = [local(acc.at[:, j, pl.ds(128, 512), :], out.at[:, :, pl.ds(128 * (j - 1), 128)]) for j in (2, 3)]

    def store(h, m):
        return [local(w.full.at[h, m, pl.ds(k * S, S), :], probe_out.at[h, m, :, pl.ds(k * H, H)]) for k in range(2)]

    done += store(core, 0)
    next(chains[1])
    arrived(middle + corners)
    for ch in range(2):
        acc[ch, 1, 128:640] += w.xl[ch]
        acc[ch, 4, 128:640] += w.xr[ch]
    done += [local(acc.at[:, j, pl.ds(128, 512), :], out.at[:, :, pl.ds(128 * (j - 1), 128)]) for j in (1, 4)]
    next(chains[0])
    done += store(1 - core, 0)
    next(chains[1])
    done += store(core, 1)
    next(chains[1])
    done += store(1 - core, 1)
    for copy in done:
        copy.wait()
    send.finish()


def place_kernel(a, b, out_a, out_b, held_a, held_b, sem):
    parts = [((n // 4, pl.ds(128 * (n % 4), 128)), a, held_a, out_a) for n in range(8)]
    parts += [((n // 2, n % 2), b, held_b, out_b) for n in range(4)]
    first = [pltpu.make_async_copy(src.at[at], held.at[at], sem.at[0, n]) for n, (at, src, held, dst) in enumerate(parts)]
    second = [pltpu.make_async_copy(held.at[at], dst.at[at], sem.at[1, n]) for n, (at, src, held, dst) in enumerate(parts)]
    for copy in first:
        copy.start()
    for one, two in zip(first, second):
        one.wait()
        two.start()
    for copy in second:
        copy.wait()


def placed(a, b):
    anywhere = pl.BlockSpec(memory_space=pl.ANY)
    return pl.pallas_call(
        place_kernel,
        out_shape=(jax.ShapeDtypeStruct(a.shape, F32), jax.ShapeDtypeStruct(b.shape, F32)),
        in_specs=[anywhere] * 2,
        out_specs=(anywhere, anywhere),
        scratch_shapes=[pltpu.VMEM(a.shape, F32), pltpu.VMEM(b.shape, F32), pltpu.SemaphoreType.DMA((2, 12))],
        compiler_params=pltpu.CompilerParams(vmem_limit_bytes=60 * 2**20),
    )(a, b)


def body(object_field, probe, patterns, offsets):
    tables_in = [jnp.asarray(t) for t in tables(S)]
    anywhere = pl.BlockSpec(memory_space=pl.ANY)
    return placed(*pl.pallas_call(
        kernel,
        out_shape=(jax.ShapeDtypeStruct(object_field.shape, F32), jax.ShapeDtypeStruct(probe.shape, F32)),
        in_specs=[pl.BlockSpec(memory_space=pltpu.SMEM)] + [anywhere] * 8,
        out_specs=(anywhere, anywhere),
        scratch_shapes=[pltpu.VMEM(*v) for v in SCRATCH.values()] + [
            pltpu.SemaphoreType.DMA((LOCALS,)), pltpu.SemaphoreType.DMA((REMOTES,)), pltpu.SemaphoreType.DMA((REMOTES,))],
        compiler_params=pltpu.CompilerParams(collective_id=0, has_side_effects=True, vmem_limit_bytes=58 * 2**20),
    )(offsets, object_field, probe, patterns, *tables_in))


def solution(mesh):
    in_specs = (P(None, "row", "col"), P(), P(("row", "col"), None, None), P(("row", "col"), None))
    out_specs = (P(None, "row", "col"), P())
    return jax.shard_map(body, mesh=mesh, in_specs=in_specs, out_specs=out_specs, check_vma=False)
```

```python
import functools
import math

import jax
import jax.numpy as jnp
import ml_dtypes
import numpy as np
from jax import lax
from jax.experimental import pallas as pl
from jax.experimental.pallas import tpu as pltpu
from jax.sharding import PartitionSpec as P

BF = jnp.bfloat16
F32 = jnp.float32
H = 128
S = 256
MESH = pl.DeviceIdType.MESH

def split_np(w):
    hi = w.astype(np.float32).astype(ml_dtypes.bfloat16)
    lo = (w - hi.astype(np.float64)).astype(np.float32).astype(ml_dtypes.bfloat16)
    return np.stack([hi, lo])

def tables(n):
    h = n // 2
    a = np.arange(h)
    f = 1.0 / math.sqrt(n)
    out = []
    for par in (0, 1):
        c = np.exp(-2j * np.pi * np.outer(a, 2 * a + par) / n) * f
        fwd = np.block([[c.real, c.imag], [-c.imag, c.real]])
        inv_c = np.conj(c).T
        inv = np.block([[inv_c.real, inv_c.imag], [-inv_c.imag, inv_c.real]])
        out.append((fwd, inv))
    rf = np.stack([split_np(out[p][0]) for p in (0, 1)])
    ri = np.stack([split_np(out[p][1]) for p in (0, 1)])
    cf = np.stack([split_np(out[p][0].T) for p in (0, 1)])
    ci = np.stack([split_np(out[p][1].T) for p in (0, 1)])
    perm = np.zeros((n, n), np.float32)
    for k in range(h):
        perm[2 * k, k] = 1
        perm[2 * k + 1, h + k] = 1
    return rf, cf, ci, ri, perm.astype(ml_dtypes.bfloat16)

def split(x):
    hi = x.astype(BF)
    lo = (x - hi.astype(F32)).astype(BF)
    return hi, lo


def run(steps):
    for mxu, vpu in steps:
        n = max(len(mxu), 1)
        for i in range(n):
            if i < len(mxu):
                mxu[i]()
            for t in vpu[len(vpu) * i // n: len(vpu) * (i + 1) // n]:
                t()

class Work:
    def __init__(self, **refs):
        self.__dict__.update(refs)

    def rows_dot(self, lhs, table, out):
        l = lhs[...]
        t0, t1 = table[0], table[1]
        out[...] = jnp.dot(jnp.concatenate([l, l[:, :S]], axis=1), jnp.concatenate([t0, t0, t1], axis=0), preferred_element_type=F32)

    def cols_dot(self, table, rhs, out):
        r = rhs[...]
        t0, t1 = table[0], table[1]
        out[...] = jnp.dot(jnp.concatenate([t0, t0, t1], axis=1), jnp.concatenate([r, r[:S]], axis=0), preferred_element_type=F32)

    def s1(self, m): return [lambda q=q: self.rows_dot(self.lhs1.at[m, q], self.rf.at[q], self.o1.at[m, q]) for q in range(2)]
    def s2(self, m): return [lambda q=q: self.cols_dot(self.cf.at[q], self.rhs2.at[m, q], self.o2.at[m, q]) for q in range(2)]
    def s3(self): return [lambda q=q: self.cols_dot(self.ci.at[q], self.rhs3a.at[q], self.o3.at[q]) for q in range(2)]
    def s4(self): return [lambda q=q: self.rows_dot(self.lhs4.at[q], self.ri.at[q], self.o4.at[q]) for q in range(2)]
    def s3b(self, p): return [lambda q=q: self.cols_dot(self.ci.at[q], self.rhs3b.at[p, q], self.o3b.at[p % 2, q]) for q in range(2)]
    def s4b(self, p): return [lambda q=q: self.rows_dot(self.lhs4b.at[p % 2, q], self.ri.at[q], self.o4b.at[p % 2, q]) for q in range(2)]

    def put_row(self, ref, rows, re, im):
        hi, lo = split(re)
        ref[rows, 0:H] = hi
        ref[rows, S:S + H] = lo
        hi, lo = split(im)
        ref[rows, H:S] = hi
        ref[rows, S + H:2 * S] = lo

    def put_col(self, ref, row, size, re, im):
        hi, lo = split(re)
        ref[row:row + size] = hi
        ref[S + row:S + row + size] = lo
        hi, lo = split(im)
        ref[H + row:H + row + size] = hi
        ref[S + H + row:S + H + row + size] = lo

    def v1(self, m, slot, size=16):
        def chunk(a):
            rows = slice(a, a + size)
            ar, ai = self.patch[slot, 0, rows], self.patch[slot, 1, rows]
            pr, pi_ = self.probe[0, m, rows], self.probe[1, m, rows]
            er = pr * ar - pi_ * ai
            ei = pr * ai + pi_ * ar
            self.put_row(self.lhs1.at[m, 0], rows, er[:, :H] + er[:, H:], ei[:, :H] + ei[:, H:])
            self.put_row(self.lhs1.at[m, 1], rows, er[:, :H] - er[:, H:], ei[:, :H] - ei[:, H:])
        return [functools.partial(chunk, a) for a in range(0, S, size)]

    def v2(self, m, size=16):
        def chunk(a):
            top, bot = slice(a, a + size), slice(H + a, H + a + size)
            for q in range(2):
                t, b = self.o1[m, q, top], self.o1[m, q, bot]
                p, n = t + b, t - b
                cols = slice(q * H, q * H + H)
                for par, v in ((0, p), (1, n)):
                    self.put_col(self.rhs2.at[m, par, :, cols], a, size, v[:, :H], v[:, H:])
        return [functools.partial(chunk, a) for a in range(0, H, size)]

    def vp(self, number):
        def first():
            hi, lo = split(self.pat[number])
            w = self.perm[...]
            v = jnp.dot(jnp.concatenate([hi, lo], axis=1), jnp.concatenate([w, w], axis=0), preferred_element_type=F32)
            for k in range(2):
                self.pscr[k] = v[:, k * H:(k + 1) * H]
        return [first]

    def v3(self, p, size=16):
        def chunk(q, a):
            re, im = slice(a, a + size), slice(H + a, H + a + size)
            w = [(self.o2[m, q, re], self.o2[m, q, im]) for m in range(2)]
            inten = w[0][0] * w[0][0] + w[0][1] * w[0][1] + w[1][0] * w[1][0] + w[1][1] * w[1][1]
            pat = jnp.concatenate([self.pscr[k, pl.ds(q + 2 * a, size, stride=2), :] for k in range(2)], axis=1)
            mis = 2.0 * (inten - pat)
            for m in range(2):
                self.put_col((self.rhs3b.at[p, q] if m else self.rhs3a.at[q]), a, size, w[m][0] * mis, w[m][1] * mis)
        return [functools.partial(chunk, q, a) for q in range(2) for a in range(0, H, size)]

    def v4(self, size=16):
        return self.halves(self.o3, self.lhs4, size)

    def v4b(self, p, size=16):
        return self.halves(self.o3b.at[p % 2], self.lhs4b.at[p % 2], size)

    def halves(self, o3, lhs4, size):
        def chunk(a):
            for at, op in ((a, lambda x, y: x + y), (H + a, lambda x, y: x - y)):
                re = op(o3[0, a:a + size], o3[1, a:a + size])
                im = op(o3[0, H + a:H + a + size], o3[1, H + a:H + a + size])
                for q in range(2):
                    cols = slice(q * H, q * H + H)
                    self.put_row(lhs4.at[q], slice(at, at + size), re[:, cols], im[:, cols])
        return [functools.partial(chunk, a) for a in range(0, H, size)]

    def v5(self, p, size=8):
        return self.products(0, p, self.o4, size)

    def v5b(self, p, size=8):
        return self.products(1, p, self.o4b.at[p % 2], size)

    def products(self, m, p, o4, size):
        def chunk(a):
            rows = slice(a, a + size)
            A, B = o4[0, rows], o4[1, rows]
            both = (A + B, A - B)
            for k in range(2):
                cols = slice(k * H, k * H + H)
                gr, gi = both[k][:, :H], both[k][:, H:]
                ar, ai = self.patch[p, 0, rows, cols], self.patch[p, 1, rows, cols]
                pr, pi_ = self.probe[0, m, rows, cols], self.probe[1, m, rows, cols]
                at = slice(k * S + a, k * S + a + size)
                self.pg[0, m, at] += ar * gr + ai * gi
                self.pg[1, m, at] += ar * gi - ai * gr
                re = pr * gr + pi_ * gi
                im = pr * gi - pi_ * gr
                if m == 0:
                    self.gsum[p, 0, k, rows] = re
                    self.gsum[p, 1, k, rows] = im
                else:
                    self.gsum[p, 0, k, rows] += re
                    self.gsum[p, 1, k, rows] += im
        return [functools.partial(chunk, a) for a in range(0, S, size)]

    def gather(self, slot, y, x):
        j0 = jnp.minimum(lax.shift_right_logical(x, 7), 3)
        s = x - j0 * 128
        back = (128 - s) & 127
        lane = lax.broadcasted_iota(jnp.int32, (32, 128), 1)
        for c in range(2):
            for a in range(0, S, 32):
                r = [pltpu.roll(self.ext[c, j0 + k, pl.ds(y + a, 32), :], back, 1) for k in range(3)]
                for k in range(2):
                    self.patch[slot, c, a:a + 32, k * 128:(k + 1) * 128] = jnp.where(lane < 128 - s, r[k], r[k + 1])

    def shifted(self, p, a, s):
        lane = lax.broadcasted_iota(jnp.int32, (32, 128), 1)
        for c in range(2):
            g = [pltpu.roll(self.gsum[p, c, k, a:a + 32], s & 127, 1) for k in range(2)]
            yield c, (jnp.where(lane >= s, g[0], 0.0), jnp.where(lane >= s, g[1], g[0]), jnp.where(lane >= s, 0.0, g[1]))

    def deposit(self, p, y, x):
        j0, s = column(x)

        def chunk(a):
            for c, blocks in self.shifted(p, a, s):
                for k in range(3):
                    self.acc[c, j0 + k, pl.ds(y + a, 32), :] += blocks[k]
        return [functools.partial(chunk, a) for a in range(0, S, 32)]

    def keep(self, p, x):
        j0, s = column(x)

        def chunk(a):
            for c, blocks in self.shifted(p, a, s):
                for k in range(3):
                    self.held[p - 4, c, 1 + k, PAD + a:PAD + a + 32] = blocks[k]
        return [functools.partial(chunk, a) for a in range(0, S, 32)]

    def merge(self, places, block, start, size):
        def go(t, carry):
            row = pl.multiple_of(start + t * 32, 32)
            for c in range(2):
                value = self.acc[c, block, pl.ds(row, 32), :]
                for n, (y, j0) in enumerate(places):
                    k = block - j0
                    k = jnp.where((k >= 0) & (k <= 2), k + 1, 0)
                    at = jnp.clip(row - y + PAD, 0, S + PAD)
                    value += self.held[n, c, k, pl.ds(at, 32), :]
                self.acc[c, block, pl.ds(row, 32), :] = value
            return carry
        lax.fori_loop(0, size // 32, go, 0)


PAD = 32


def column(x):
    j0 = jnp.minimum(lax.shift_right_logical(x, 7), 3)
    return j0, x - j0 * 128


def neighbours():
    rows, cols = lax.axis_size("row"), lax.axis_size("col")
    r, c = lax.axis_index("row"), lax.axis_index("col")
    left = (r, lax.rem(c + cols - 1, cols))
    right = (r, lax.rem(c + 1, cols))
    up = (lax.rem(r + rows - 1, rows), c)
    down = (lax.rem(r + 1, rows), c)
    return left, right, up, down


def greet(devices):
    barrier = pltpu.get_barrier_semaphore()
    for device in devices:
        pl.semaphore_signal(barrier, inc=1, device_id=device, device_id_type=MESH)


def met(devices):
    pl.semaphore_wait(pltpu.get_barrier_semaphore(), len(devices))


class Sender:
    def __init__(self, send_sem, recv_sem):
        self.send_sem, self.recv_sem, self.copies = send_sem, recv_sem, []

    def __call__(self, src, dst, device, start=True):
        n = len(self.copies)
        copy = pltpu.make_async_remote_copy(
            src_ref=src, dst_ref=dst, send_sem=self.send_sem.at[n], recv_sem=self.recv_sem.at[n],
            device_id=device, device_id_type=MESH)
        if start:
            copy.start()
        self.copies.append(copy)
        return copy

    def finish(self):
        for copy in self.copies:
            copy.wait_send()


class Local:
    def __init__(self, sem):
        self.sem, self.count = sem, 0

    def __call__(self, src, dst):
        copy = pltpu.make_async_copy(src, dst, self.sem.at[self.count])
        self.count += 1
        copy.start()
        return copy


def arrived(copies):
    for copy in copies:
        copy.wait_recv()


SCRATCH = dict(
    ext=((2, 6, 768, H), F32), acc=((2, 6, 768, H), F32), probe=((2, 2, S, S), F32), pat=((8, S, S), F32),
    rf=((2, 2, S, S), BF), cf=((2, 2, S, S), BF), ci=((2, 2, S, S), BF), ri=((2, 2, S, S), BF), perm=((S, S), BF),
    pg=((2, 2, 512, H), F32), patch=((8, 2, S, S), F32), lhs1=((2, 2, S, 2 * S), BF), o1=((2, 2, S, S), F32), rhs2=((2, 2, 2 * S, S), BF),
    o2=((2, 2, S, S), F32), rhs3a=((2, 2 * S, S), BF), rhs3b=((8, 2, 2 * S, S), BF), o3=((2, S, S), F32), lhs4=((2, S, 2 * S), BF), o4=((2, S, S), F32),
    o3b=((2, 2, S, S), F32), lhs4b=((2, 2, S, 2 * S), BF), o4b=((2, 2, S, S), F32),
    pscr=((2, S, H), F32), gsum=((8, 2, 2, S, H), F32), held=((4, 2, 4, S + 2 * PAD, H), F32),
    ytop=((2, 6, H, H), F32), ybot=((2, 6, H, H), F32), xl=((2, 512, H), F32), xr=((2, 512, H), F32),
    pair=((2, 512, H), F32), part=((2, 512, H), F32), r1=((2, 15, 32, H), F32), r2=((2, 4, 32, H), F32), full=((2, 2, 512, H), F32))
REMOTES = 6 + 2 + 4 + 4 + 2 + 2 + 4 + 2 * 35
LOCALS = 4 + 7 + 4 + 8


def kernel(off, obj, probe_in, pat_in, rf_in, cf_in, ci_in, ri_in, perm_in, out, probe_out, *scr):
    refs = dict(zip(SCRATCH, scr))
    w = Work(**refs)
    ext, acc, pg = w.ext, w.acc, w.pg
    local_sem, send_sem, recv_sem = scr[len(SCRATCH):]
    r, c = lax.axis_index("row"), lax.axis_index("col")
    rows, cols = lax.axis_size("row"), lax.axis_size("col")
    y, core, z, x = lax.div(r, 2), lax.rem(r, 2), lax.div(c, 4), lax.rem(c, 4)
    left, right, up, down = neighbours()
    other = (r + 1 - 2 * core, c)
    turn = lambda i, d: lax.rem(i + d, 4)
    plane = [(turn(z, a), turn(x, b)) for a in range(4) for b in range(4) if a or b]
    planes = [(r, a * 4 + b) for a, b in plane]
    line = [(turn(y, d) * 2 + core, c) for d in (1, 2, 3)]
    everyone = [left, right, up, down, other] + planes + line
    greet(everyone)
    local = Local(local_sem)
    own = [local(obj.at[:, :, pl.ds(128 * j, 128)], ext.at[:, 1 + j, pl.ds(128, 512), :]) for j in range(4)]
    own += [local(a, b) for a, b in ((probe_in, w.probe), (rf_in, w.rf), (cf_in, w.cf), (perm_in, w.perm), (pat_in, w.pat), (ci_in, w.ci), (ri_in, w.ri))]
    for copy in own[:4]:
        copy.wait()
    met(everyone)
    send = Sender(send_sem, recv_sem)

    def side(start, size):
        rows_there = pl.ds(start, size)
        return (send(ext.at[:, 1, rows_there, :], ext.at[:, 5, rows_there, :], left),
                send(ext.at[:, 4, rows_there, :], ext.at[:, 0, rows_there, :], right))

    inner = pl.ds(1, 4)
    across = [side(504, 136)]
    top = [send(ext.at[:, inner, pl.ds(512, 128), :], ext.at[:, inner, pl.ds(0, 128), :], down)]
    across.append(side(128, 128))
    bottom = [send(ext.at[:, inner, pl.ds(128, 128), :], ext.at[:, inner, pl.ds(640, 128), :], up)]
    across.append(side(256, 248))
    acc[...] = jnp.zeros_like(acc)
    pg[...] = jnp.zeros_like(pg)
    w.held[:, :, 0] = jnp.zeros((4, 2, S + 2 * PAD, H), F32)
    w.held[:, :, 1:4, 0:PAD] = jnp.zeros((4, 2, 3, PAD, H), F32)
    w.held[:, :, 1:4, S + PAD:] = jnp.zeros((4, 2, 3, PAD, H), F32)

    for k, (place, target, device, group) in enumerate(((512, 0, down, top), (128, 640, up, bottom))):
        for block, copy in zip((5, 0), across[k]):
            copy.wait_recv()
            group.append(send(ext.at[:, block, pl.ds(place, 128), :], ext.at[:, block, pl.ds(target, 128), :], device))

    base_y, base_x = r * 512 - 128, c * 512 - 128
    low_y = jnp.maximum(base_y, 0) - base_y
    low_x = jnp.maximum(base_x, 0) - base_x
    high_y = jnp.minimum(base_y + 511, rows * 512 - S) - base_y
    high_x = jnp.minimum(base_x + 511, cols * 512 - S) - base_x

    def corner(k):
        return jnp.where(k < 2, low_y, high_y), jnp.where(lax.rem(k, 2) == 0, low_x, high_x)

    def given(k):
        return jnp.clip(off[0, k] - base_y, 0, 512), jnp.clip(off[1, k] - base_x, 0, 512)

    def number(k):
        cy, cx = corner(k)
        found = 0
        for n in range(1, 4):
            gy, gx = given(n)
            found = jnp.where((gy == cy) & (gx == cx), n, found)
        return jnp.where(k < 4, found, k)

    for copy in own[4:]:
        copy.wait()
    arrived(top)

    @pl.when(r == 0)
    def _():
        arrived(across[2])

    for k in range(2):
        w.gather(k, *corner(jnp.int32(k)))
    run([([], w.v1(0, 0)), (w.s1(0), w.v1(1, 0)), (w.s1(1), w.v2(0)), ([], w.v2(1)), (w.s2(0), w.v1(0, 1)), (w.s2(1), w.v1(1, 1))])

    piece = lambda a, b: pl.ds(pl.multiple_of((a * 4 + b) * 32, 32), 32)

    def chain(m):
        copies = [send(pg.at[1 - core, m], w.pair.at[m], other)]
        yield
        arrived(copies)
        w.part[m] = pg[core, m] + w.pair[m]
        copies = [send(w.part.at[m, piece(*to), :], w.r1.at[m, n], planes[n]) for n, to in enumerate(plane)]
        yield
        arrived(copies)
        total = w.part[m, piece(z, x), :]
        for n in range(15):
            total = total + w.r1[m, n]
        w.r2[m, y] = total
        mine = w.r2.at[m, y]
        copies = [send(mine, mine, device) for device in line]
        yield
        arrived(copies)
        w.full[core, m, piece(z, x), :] = w.r2[m, 0] + w.r2[m, 1] + w.r2[m, 2] + w.r2[m, 3]
        mine = w.full.at[core, m, piece(z, x), :]
        copies = [send(mine, mine, device) for device in planes]
        yield
        arrived(copies)
        mine = w.full.at[core, m]
        copies = [send(mine, mine, other)]
        yield
        arrived(copies)
        yield

    chains = [chain(0), chain(1)]

    run([
        (w.vp(number(jnp.int32(0))), []),
        (w.s1(0) + w.s1(1), w.v3(0)),
        (w.s3(), w.v2(0) + w.v2(1)),
        (w.s2(0), w.v4()),
        (w.s2(1), []),
    ])

    @pl.when(r != 0)
    def _():
        arrived(across[2])

    arrived(bottom)

    w.gather(2, *corner(jnp.int32(2)))
    run([(w.s4(), w.v1(0, 2) + w.v1(1, 2))])

    def step(i, carry):
        new, old = jnp.minimum(i + 1, 7), i - 2
        cy, cx = corner(new)
        gy, gx = given(new)
        w.gather(new, jnp.where(new < 4, cy, gy), jnp.where(new < 4, cx, gx))
        v5 = w.v5(old)
        run([
            (w.vp(number(i - 1)), []),
            (w.s1(0) + w.s1(1), w.v3(i - 1) + v5[:12]),
            (w.s3(), w.v2(0) + w.v2(1)),
            (w.s2(0), w.v4() + v5[12:26]),
            (w.s2(1), v5[26:] + w.v1(0, new)),
            (w.s4(), w.v1(1, new)),
        ])
        return carry

    lax.fori_loop(2, 8, step, 0)

    def settled(p):
        return w.deposit(p, *corner(jnp.int32(p))) if p < 4 else w.keep(p, given(p)[1])

    turned = [4, 5, 6, 7, 0, 1, 2, 3]
    run([(w.vp(7), []), ([], w.v3(7)), (w.s3(), w.v5(6)), (w.s3b(4), w.v4()), (w.s4(), w.v4b(4)), (w.s3b(5), w.v5(7))])
    next(chains[0])
    run([(w.s4b(4), w.v4b(5)), (w.s3b(6), w.v5b(4) + settled(4)), (w.s4b(5), w.v4b(6))])
    next(chains[0])
    places = [(given(k)[0], column(given(k)[1])[0]) for k in range(4, 8)]
    outer = (r == 0) | (r == rows - 1)
    middle = []
    for n in range(3, 8):
        old = turned[n - 2]
        run([(w.s3b(turned[n]), w.v5b(old) + settled(old)), (w.s4b(turned[n - 1]), w.v4b(turned[n]))])
        if n == 5:
            for block, into, device in ((0, w.xr, left), (5, w.xl, right)):
                w.merge(places, block, 256, 256)
                middle.append(send(acc.at[:, block, pl.ds(256, 248), :], into.at[:, pl.ds(128, 248), :], device, start=False))

            @pl.when(jnp.logical_not(outer))
            def _():
                for copy in middle:
                    copy.start()

            for block in (0, 5):
                w.merge(places, block, 0, 128)
                w.merge(places, block, 640, 128)
    run([(w.s4b(3), w.v5b(2) + settled(2))])
    run([([], w.v5b(3))])
    next(chains[1])
    next(chains[0])
    run([([], settled(3))])
    next(chains[1])

    @pl.when(outer)
    def _():
        for copy in middle:
            copy.start()

    sides = []
    for block in (0, 5):
        sides.append((send(acc.at[:, block, pl.ds(0, 128), :], w.ybot.at[:, block], up),
                      send(acc.at[:, block, pl.ds(640, 128), :], w.ytop.at[:, block], down)))
    for j in range(1, 5):
        w.merge(places, j, 0, 128)
        w.merge(places, j, 640, 128)
    along = [send(acc.at[:, inner, pl.ds(0, 128), :], w.ybot.at[:, inner], up),
             send(acc.at[:, inner, pl.ds(640, 128), :], w.ytop.at[:, inner], down)]
    for block in (0, 5):
        w.merge(places, block, 128, 128)
        w.merge(places, block, 512, 128)
    corners = []
    for block, got in zip((0, 5), sides):
        arrived(got)
        for row, came, start, size in ((128, w.ytop, 128, 128), (512, w.ybot, 504, 136)):
            for ch in range(2):
                acc[ch, block, row:row + 128] += came[ch, block]
            into, device = (w.xr, left) if block == 0 else (w.xl, right)
            corners.append(send(acc.at[:, block, pl.ds(start, size), :], into.at[:, pl.ds(start - 128, size), :], device))
    next(chains[0])
    for j in range(1, 5):
        w.merge(places, j, 128, 512)
    next(chains[1])
    next(chains[0])
    arrived(along)
    for ch in range(2):
        for j in range(1, 5):
            acc[ch, j, 128:256] += w.ytop[ch, j]
            acc[ch, j, 512:640] += w.ybot[ch, j]
    done = [local(acc.at[:, j, pl.ds(128, 512), :], out.at[:, :, pl.ds(128 * (j - 1), 128)]) for j in (2, 3)]

    def store(h, m):
        return [local(w.full.at[h, m, pl.ds(k * S, S), :], probe_out.at[h, m, :, pl.ds(k * H, H)]) for k in range(2)]

    done += store(core, 0)
    next(chains[1])
    arrived(middle + corners)
    for ch in range(2):
        acc[ch, 1, 128:640] += w.xl[ch]
        acc[ch, 4, 128:640] += w.xr[ch]
    done += [local(acc.at[:, j, pl.ds(128, 512), :], out.at[:, :, pl.ds(128 * (j - 1), 128)]) for j in (1, 4)]
    next(chains[0])
    done += store(1 - core, 0)
    next(chains[1])
    done += store(core, 1)
    next(chains[1])
    done += store(1 - core, 1)
    for copy in done:
        copy.wait()
    send.finish()


def place_kernel(a, b, out_a, out_b, held_a, held_b, sem):
    parts = [((n // 4, pl.ds(128 * (n % 4), 128)), a, held_a, out_a) for n in range(8)]
    parts += [((n // 2, n % 2), b, held_b, out_b) for n in range(4)]
    first = [pltpu.make_async_copy(src.at[at], held.at[at], sem.at[0, n]) for n, (at, src, held, dst) in enumerate(parts)]
    second = [pltpu.make_async_copy(held.at[at], dst.at[at], sem.at[1, n]) for n, (at, src, held, dst) in enumerate(parts)]
    for copy in first:
        copy.start()
    for one, two in zip(first, second):
        one.wait()
        two.start()
    for copy in second:
        copy.wait()


def placed(a, b):
    anywhere = pl.BlockSpec(memory_space=pl.ANY)
    return pl.pallas_call(
        place_kernel,
        out_shape=(jax.ShapeDtypeStruct(a.shape, F32), jax.ShapeDtypeStruct(b.shape, F32)),
        in_specs=[anywhere] * 2,
        out_specs=(anywhere, anywhere),
        scratch_shapes=[pltpu.VMEM(a.shape, F32), pltpu.VMEM(b.shape, F32), pltpu.SemaphoreType.DMA((2, 12))],
        compiler_params=pltpu.CompilerParams(vmem_limit_bytes=60 * 2**20),
    )(a, b)


def body(object_field, probe, patterns, offsets):
    tables_in = [jnp.asarray(t) for t in tables(S)]
    anywhere = pl.BlockSpec(memory_space=pl.ANY)
    return placed(*pl.pallas_call(
        kernel,
        out_shape=(jax.ShapeDtypeStruct(object_field.shape, F32), jax.ShapeDtypeStruct(probe.shape, F32)),
        in_specs=[pl.BlockSpec(memory_space=pltpu.SMEM)] + [anywhere] * 8,
        out_specs=(anywhere, anywhere),
        scratch_shapes=[pltpu.VMEM(*v) for v in SCRATCH.values()] + [
            pltpu.SemaphoreType.DMA((LOCALS,)), pltpu.SemaphoreType.DMA((REMOTES,)), pltpu.SemaphoreType.DMA((REMOTES,))],
        compiler_params=pltpu.CompilerParams(collective_id=0, has_side_effects=True, vmem_limit_bytes=58 * 2**20),
    )(offsets.T, object_field, probe, patterns, *tables_in))


def solution(mesh):
    in_specs = (P(None, "row", "col"), P(), P(("row", "col"), None, None), P(("row", "col"), None))
    out_specs = (P(None, "row", "col"), P())
    return jax.shard_map(body, mesh=mesh, in_specs=in_specs, out_specs=out_specs, check_vma=False)
```

```python
import functools
import math

import jax
import jax.numpy as jnp
import ml_dtypes
import numpy as np
from jax import lax
from jax.experimental import pallas as pl
from jax.experimental.pallas import tpu as pltpu
from jax.sharding import PartitionSpec as P

BF = jnp.bfloat16
F32 = jnp.float32
H = 128
S = 256
MESH = pl.DeviceIdType.MESH

def split_np(w):
    hi = w.astype(np.float32).astype(ml_dtypes.bfloat16)
    lo = (w - hi.astype(np.float64)).astype(np.float32).astype(ml_dtypes.bfloat16)
    return np.stack([hi, lo])

def tables(n):
    h = n // 2
    a = np.arange(h)
    f = 1.0 / math.sqrt(n)
    out = []
    for par in (0, 1):
        c = np.exp(-2j * np.pi * np.outer(a, 2 * a + par) / n) * f
        fwd = np.block([[c.real, c.imag], [-c.imag, c.real]])
        inv_c = np.conj(c).T
        inv = np.block([[inv_c.real, inv_c.imag], [-inv_c.imag, inv_c.real]])
        out.append((fwd, inv))
    rf = np.stack([split_np(out[p][0]) for p in (0, 1)])
    ri = np.stack([split_np(out[p][1]) for p in (0, 1)])
    cf = np.stack([split_np(out[p][0].T) for p in (0, 1)])
    ci = np.stack([split_np(out[p][1].T) for p in (0, 1)])
    perm = np.zeros((n, n), np.float32)
    for k in range(h):
        perm[2 * k, k] = 1
        perm[2 * k + 1, h + k] = 1
    return rf, cf, ci, ri, perm.astype(ml_dtypes.bfloat16)

def split(x):
    hi = x.astype(BF)
    lo = (x - hi.astype(F32)).astype(BF)
    return hi, lo


def run(steps):
    for mxu, vpu in steps:
        n = max(len(mxu), 1)
        for i in range(n):
            if i < len(mxu):
                mxu[i]()
            for t in vpu[len(vpu) * i // n: len(vpu) * (i + 1) // n]:
                t()

class Work:
    def __init__(self, **refs):
        self.__dict__.update(refs)

    def rows_dot(self, lhs, table, out):
        l = lhs[...]
        t0, t1 = table[0], table[1]
        out[...] = jnp.dot(jnp.concatenate([l, l[:, :S]], axis=1), jnp.concatenate([t0, t0, t1], axis=0), preferred_element_type=F32)

    def cols_dot(self, table, rhs, out):
        r = rhs[...]
        t0, t1 = table[0], table[1]
        out[...] = jnp.dot(jnp.concatenate([t0, t0, t1], axis=1), jnp.concatenate([r, r[:S]], axis=0), preferred_element_type=F32)

    def s1(self, m): return [lambda q=q: self.rows_dot(self.lhs1.at[m, q], self.rf.at[q], self.o1.at[m, q]) for q in range(2)]
    def s2(self, m): return [lambda q=q: self.cols_dot(self.cf.at[q], self.rhs2.at[m, q], self.o2.at[m, q]) for q in range(2)]
    def s3(self): return [lambda q=q: self.cols_dot(self.ci.at[q], self.rhs3a.at[q], self.o3.at[q]) for q in range(2)]
    def s4(self): return [lambda q=q: self.rows_dot(self.lhs4.at[q], self.ri.at[q], self.o4.at[q]) for q in range(2)]
    def s3b(self, p): return [lambda q=q: self.cols_dot(self.ci.at[q], self.rhs3b.at[p, q], self.o3b.at[p % 2, q]) for q in range(2)]
    def s4b(self, p): return [lambda q=q: self.rows_dot(self.lhs4b.at[p % 2, q], self.ri.at[q], self.o4b.at[p % 2, q]) for q in range(2)]

    def put_row(self, ref, rows, re, im):
        hi, lo = split(re)
        ref[rows, 0:H] = hi
        ref[rows, S:S + H] = lo
        hi, lo = split(im)
        ref[rows, H:S] = hi
        ref[rows, S + H:2 * S] = lo

    def put_col(self, ref, row, size, re, im):
        hi, lo = split(re)
        ref[row:row + size] = hi
        ref[S + row:S + row + size] = lo
        hi, lo = split(im)
        ref[H + row:H + row + size] = hi
        ref[S + H + row:S + H + row + size] = lo

    def v1(self, m, slot, size=16):
        def chunk(a):
            rows = slice(a, a + size)
            ar, ai = self.patch[slot, 0, rows], self.patch[slot, 1, rows]
            pr, pi_ = self.probe[0, m, rows], self.probe[1, m, rows]
            er = pr * ar - pi_ * ai
            ei = pr * ai + pi_ * ar
            self.put_row(self.lhs1.at[m, 0], rows, er[:, :H] + er[:, H:], ei[:, :H] + ei[:, H:])
            self.put_row(self.lhs1.at[m, 1], rows, er[:, :H] - er[:, H:], ei[:, :H] - ei[:, H:])
        return [functools.partial(chunk, a) for a in range(0, S, size)]

    def v2(self, m, size=16):
        def chunk(a):
            top, bot = slice(a, a + size), slice(H + a, H + a + size)
            for q in range(2):
                t, b = self.o1[m, q, top], self.o1[m, q, bot]
                p, n = t + b, t - b
                cols = slice(q * H, q * H + H)
                for par, v in ((0, p), (1, n)):
                    self.put_col(self.rhs2.at[m, par, :, cols], a, size, v[:, :H], v[:, H:])
        return [functools.partial(chunk, a) for a in range(0, H, size)]

    def vp(self, number):
        def first():
            hi, lo = split(self.pat[number])
            w = self.perm[...]
            v = jnp.dot(jnp.concatenate([hi, lo], axis=1), jnp.concatenate([w, w], axis=0), preferred_element_type=F32)
            for k in range(2):
                self.pscr[k] = v[:, k * H:(k + 1) * H]
        return [first]

    def v3(self, p, size=16):
        def chunk(q, a):
            re, im = slice(a, a + size), slice(H + a, H + a + size)
            w = [(self.o2[m, q, re], self.o2[m, q, im]) for m in range(2)]
            inten = w[0][0] * w[0][0] + w[0][1] * w[0][1] + w[1][0] * w[1][0] + w[1][1] * w[1][1]
            pat = jnp.concatenate([self.pscr[k, pl.ds(q + 2 * a, size, stride=2), :] for k in range(2)], axis=1)
            mis = 2.0 * (inten - pat)
            for m in range(2):
                self.put_col((self.rhs3b.at[p, q] if m else self.rhs3a.at[q]), a, size, w[m][0] * mis, w[m][1] * mis)
        return [functools.partial(chunk, q, a) for q in range(2) for a in range(0, H, size)]

    def v4(self, size=16):
        return self.halves(self.o3, self.lhs4, size)

    def v4b(self, p, size=16):
        return self.halves(self.o3b.at[p % 2], self.lhs4b.at[p % 2], size)

    def halves(self, o3, lhs4, size):
        def chunk(a):
            for at, op in ((a, lambda x, y: x + y), (H + a, lambda x, y: x - y)):
                re = op(o3[0, a:a + size], o3[1, a:a + size])
                im = op(o3[0, H + a:H + a + size], o3[1, H + a:H + a + size])
                for q in range(2):
                    cols = slice(q * H, q * H + H)
                    self.put_row(lhs4.at[q], slice(at, at + size), re[:, cols], im[:, cols])
        return [functools.partial(chunk, a) for a in range(0, H, size)]

    def v5(self, p, size=8):
        return self.products(0, p, self.o4, size)

    def v5b(self, p, size=8):
        return self.products(1, p, self.o4b.at[p % 2], size)

    def products(self, m, p, o4, size):
        def chunk(a):
            rows = slice(a, a + size)
            A, B = o4[0, rows], o4[1, rows]
            both = (A + B, A - B)
            for k in range(2):
                cols = slice(k * H, k * H + H)
                gr, gi = both[k][:, :H], both[k][:, H:]
                ar, ai = self.patch[p, 0, rows, cols], self.patch[p, 1, rows, cols]
                pr, pi_ = self.probe[0, m, rows, cols], self.probe[1, m, rows, cols]
                at = slice(k * S + a, k * S + a + size)
                self.pg[0, m, at] += ar * gr + ai * gi
                self.pg[1, m, at] += ar * gi - ai * gr
                re = pr * gr + pi_ * gi
                im = pr * gi - pi_ * gr
                if m == 0:
                    self.gsum[p, 0, k, rows] = re
                    self.gsum[p, 1, k, rows] = im
                else:
                    self.gsum[p, 0, k, rows] += re
                    self.gsum[p, 1, k, rows] += im
        return [functools.partial(chunk, a) for a in range(0, S, size)]

    def gather(self, slot, y, x):
        j0 = jnp.minimum(lax.shift_right_logical(x, 7), 3)
        s = x - j0 * 128
        back = (128 - s) & 127
        lane = lax.broadcasted_iota(jnp.int32, (32, 128), 1)
        for c in range(2):
            for a in range(0, S, 32):
                r = [pltpu.roll(self.ext[c, j0 + k, pl.ds(y + a, 32), :], back, 1) for k in range(3)]
                for k in range(2):
                    self.patch[slot, c, a:a + 32, k * 128:(k + 1) * 128] = jnp.where(lane < 128 - s, r[k], r[k + 1])

    def shifted(self, p, a, s):
        lane = lax.broadcasted_iota(jnp.int32, (32, 128), 1)
        for c in range(2):
            g = [pltpu.roll(self.gsum[p, c, k, a:a + 32], s & 127, 1) for k in range(2)]
            yield c, (jnp.where(lane >= s, g[0], 0.0), jnp.where(lane >= s, g[1], g[0]), jnp.where(lane >= s, 0.0, g[1]))

    def deposit(self, p, y, x):
        j0, s = column(x)

        def chunk(a):
            for c, blocks in self.shifted(p, a, s):
                for k in range(3):
                    self.acc[c, j0 + k, pl.ds(y + a, 32), :] += blocks[k]
        return [functools.partial(chunk, a) for a in range(0, S, 32)]

    def keep(self, p, x):
        j0, s = column(x)

        def chunk(a):
            for c, blocks in self.shifted(p, a, s):
                for k in range(3):
                    self.held[p - 4, c, 1 + k, PAD + a:PAD + a + 32] = blocks[k]
        return [functools.partial(chunk, a) for a in range(0, S, 32)]

    def merge(self, places, block, start, size):
        def go(t, carry):
            row = pl.multiple_of(start + t * 32, 32)
            for c in range(2):
                value = self.acc[c, block, pl.ds(row, 32), :]
                for n, (y, j0) in enumerate(places):
                    k = block - j0
                    k = jnp.where((k >= 0) & (k <= 2), k + 1, 0)
                    at = jnp.clip(row - y + PAD, 0, S + PAD)
                    value += self.held[n, c, k, pl.ds(at, 32), :]
                self.acc[c, block, pl.ds(row, 32), :] = value
            return carry
        lax.fori_loop(0, size // 32, go, 0)


PAD = 32


def column(x):
    j0 = jnp.minimum(lax.shift_right_logical(x, 7), 3)
    return j0, x - j0 * 128


def neighbours():
    rows, cols = lax.axis_size("row"), lax.axis_size("col")
    r, c = lax.axis_index("row"), lax.axis_index("col")
    left = (r, lax.rem(c + cols - 1, cols))
    right = (r, lax.rem(c + 1, cols))
    up = (lax.rem(r + rows - 1, rows), c)
    down = (lax.rem(r + 1, rows), c)
    return left, right, up, down


def greet(devices):
    barrier = pltpu.get_barrier_semaphore()
    for device in devices:
        pl.semaphore_signal(barrier, inc=1, device_id=device, device_id_type=MESH)


def met(devices):
    pl.semaphore_wait(pltpu.get_barrier_semaphore(), len(devices))


class Sender:
    def __init__(self, send_sem, recv_sem):
        self.send_sem, self.recv_sem, self.copies = send_sem, recv_sem, []

    def __call__(self, src, dst, device, start=True):
        n = len(self.copies)
        copy = pltpu.make_async_remote_copy(
            src_ref=src, dst_ref=dst, send_sem=self.send_sem.at[n], recv_sem=self.recv_sem.at[n],
            device_id=device, device_id_type=MESH)
        if start:
            copy.start()
        self.copies.append(copy)
        return copy

    def finish(self):
        for copy in self.copies:
            copy.wait_send()


class Local:
    def __init__(self, sem):
        self.sem, self.count = sem, 0

    def __call__(self, src, dst):
        copy = pltpu.make_async_copy(src, dst, self.sem.at[self.count])
        self.count += 1
        copy.start()
        return copy


def arrived(copies):
    for copy in copies:
        copy.wait_recv()


SCRATCH = dict(
    ext=((2, 6, 768, H), F32), acc=((2, 6, 768, H), F32), probe=((2, 2, S, S), F32), pat=((8, S, S), F32),
    rf=((2, 2, S, S), BF), cf=((2, 2, S, S), BF), ci=((2, 2, S, S), BF), ri=((2, 2, S, S), BF), perm=((S, S), BF),
    pg=((2, 2, 512, H), F32), patch=((8, 2, S, S), F32), lhs1=((2, 2, S, 2 * S), BF), o1=((2, 2, S, S), F32), rhs2=((2, 2, 2 * S, S), BF),
    o2=((2, 2, S, S), F32), rhs3a=((2, 2 * S, S), BF), rhs3b=((8, 2, 2 * S, S), BF), o3=((2, S, S), F32), lhs4=((2, S, 2 * S), BF), o4=((2, S, S), F32),
    o3b=((2, 2, S, S), F32), lhs4b=((2, 2, S, 2 * S), BF), o4b=((2, 2, S, S), F32),
    pscr=((2, S, H), F32), gsum=((8, 2, 2, S, H), F32), held=((4, 2, 4, S + 2 * PAD, H), F32),
    ytop=((2, 6, H, H), F32), ybot=((2, 6, H, H), F32), xl=((2, 512, H), F32), xr=((2, 512, H), F32),
    pair=((2, 512, H), F32), part=((2, 512, H), F32), r1=((2, 15, 32, H), F32), r2=((2, 4, 32, H), F32), full=((2, 2, 512, H), F32))
REMOTES = 6 + 2 + 4 + 4 + 2 + 2 + 4 + 2 * 35
LOCALS = 4 + 7 + 4 + 8


def kernel(off, obj, probe_in, pat_in, rf_in, cf_in, ci_in, ri_in, perm_in, out, probe_out, *scr):
    refs = dict(zip(SCRATCH, scr))
    w = Work(**refs)
    ext, acc, pg = w.ext, w.acc, w.pg
    local_sem, send_sem, recv_sem = scr[len(SCRATCH):]
    r, c = lax.axis_index("row"), lax.axis_index("col")
    rows, cols = lax.axis_size("row"), lax.axis_size("col")
    y, core, z, x = lax.div(r, 2), lax.rem(r, 2), lax.div(c, 4), lax.rem(c, 4)
    left, right, up, down = neighbours()
    other = (r + 1 - 2 * core, c)
    turn = lambda i, d: lax.rem(i + d, 4)
    plane = [(turn(y, a), turn(x, b)) for a in range(4) for b in range(4) if a or b]
    planes = [(a * 2 + core, z * 4 + b) for a, b in plane]
    line = [(r, turn(z, d) * 4 + x) for d in (1, 2, 3)]
    everyone = [left, right, up, down, other] + planes + line
    greet(everyone)
    local = Local(local_sem)
    own = [local(obj.at[:, :, pl.ds(128 * j, 128)], ext.at[:, 1 + j, pl.ds(128, 512), :]) for j in range(4)]
    own += [local(a, b) for a, b in ((probe_in, w.probe), (rf_in, w.rf), (cf_in, w.cf), (perm_in, w.perm), (pat_in, w.pat), (ci_in, w.ci), (ri_in, w.ri))]
    for copy in own[:4]:
        copy.wait()
    met(everyone)
    send = Sender(send_sem, recv_sem)

    def side(start, size):
        rows_there = pl.ds(start, size)
        return (send(ext.at[:, 1, rows_there, :], ext.at[:, 5, rows_there, :], left),
                send(ext.at[:, 4, rows_there, :], ext.at[:, 0, rows_there, :], right))

    inner = pl.ds(1, 4)
    across = [side(504, 136)]
    top = [send(ext.at[:, inner, pl.ds(512, 128), :], ext.at[:, inner, pl.ds(0, 128), :], down)]
    across.append(side(128, 128))
    bottom = [send(ext.at[:, inner, pl.ds(128, 128), :], ext.at[:, inner, pl.ds(640, 128), :], up)]
    across.append(side(256, 248))
    acc[...] = jnp.zeros_like(acc)
    pg[...] = jnp.zeros_like(pg)
    w.held[:, :, 0] = jnp.zeros((4, 2, S + 2 * PAD, H), F32)
    w.held[:, :, 1:4, 0:PAD] = jnp.zeros((4, 2, 3, PAD, H), F32)
    w.held[:, :, 1:4, S + PAD:] = jnp.zeros((4, 2, 3, PAD, H), F32)

    for k, (place, target, device, group) in enumerate(((512, 0, down, top), (128, 640, up, bottom))):
        for block, copy in zip((5, 0), across[k]):
            copy.wait_recv()
            group.append(send(ext.at[:, block, pl.ds(place, 128), :], ext.at[:, block, pl.ds(target, 128), :], device))

    base_y, base_x = r * 512 - 128, c * 512 - 128
    low_y = jnp.maximum(base_y, 0) - base_y
    low_x = jnp.maximum(base_x, 0) - base_x
    high_y = jnp.minimum(base_y + 511, rows * 512 - S) - base_y
    high_x = jnp.minimum(base_x + 511, cols * 512 - S) - base_x

    def corner(k):
        return jnp.where(k < 2, low_y, high_y), jnp.where(lax.rem(k, 2) == 0, low_x, high_x)

    def given(k):
        return jnp.clip(off[0, k] - base_y, 0, 512), jnp.clip(off[1, k] - base_x, 0, 512)

    def number(k):
        cy, cx = corner(k)
        found = 0
        for n in range(1, 4):
            gy, gx = given(n)
            found = jnp.where((gy == cy) & (gx == cx), n, found)
        return jnp.where(k < 4, found, k)

    for copy in own[4:]:
        copy.wait()
    arrived(top)

    @pl.when(r == 0)
    def _():
        arrived(across[2])

    for k in range(2):
        w.gather(k, *corner(jnp.int32(k)))
    run([([], w.v1(0, 0)), (w.s1(0), w.v1(1, 0)), (w.s1(1), w.v2(0)), ([], w.v2(1)), (w.s2(0), w.v1(0, 1)), (w.s2(1), w.v1(1, 1))])

    piece = lambda a, b: pl.ds(pl.multiple_of((a * 4 + b) * 32, 32), 32)

    def chain(m):
        copies = [send(pg.at[1 - core, m], w.pair.at[m], other)]
        yield
        arrived(copies)
        w.part[m] = pg[core, m] + w.pair[m]
        copies = [send(w.part.at[m, piece(*to), :], w.r1.at[m, n], planes[n]) for n, to in enumerate(plane)]
        yield
        arrived(copies)
        total = w.part[m, piece(y, x), :]
        for n in range(15):
            total = total + w.r1[m, n]
        w.r2[m, z] = total
        mine = w.r2.at[m, z]
        copies = [send(mine, mine, device) for device in line]
        yield
        arrived(copies)
        w.full[core, m, piece(y, x), :] = w.r2[m, 0] + w.r2[m, 1] + w.r2[m, 2] + w.r2[m, 3]
        mine = w.full.at[core, m, piece(y, x), :]
        copies = [send(mine, mine, device) for device in planes]
        yield
        arrived(copies)
        mine = w.full.at[core, m]
        copies = [send(mine, mine, other)]
        yield
        arrived(copies)
        yield

    chains = [chain(0), chain(1)]

    run([
        (w.vp(number(jnp.int32(0))), []),
        (w.s1(0) + w.s1(1), w.v3(0)),
        (w.s3(), w.v2(0) + w.v2(1)),
        (w.s2(0), w.v4()),
        (w.s2(1), []),
    ])

    @pl.when(r != 0)
    def _():
        arrived(across[2])

    arrived(bottom)

    w.gather(2, *corner(jnp.int32(2)))
    run([(w.s4(), w.v1(0, 2) + w.v1(1, 2))])

    def step(i, carry):
        new, old = jnp.minimum(i + 1, 7), i - 2
        cy, cx = corner(new)
        gy, gx = given(new)
        w.gather(new, jnp.where(new < 4, cy, gy), jnp.where(new < 4, cx, gx))
        v5 = w.v5(old)
        run([
            (w.vp(number(i - 1)), []),
            (w.s1(0) + w.s1(1), w.v3(i - 1) + v5[:12]),
            (w.s3(), w.v2(0) + w.v2(1)),
            (w.s2(0), w.v4() + v5[12:26]),
            (w.s2(1), v5[26:] + w.v1(0, new)),
            (w.s4(), w.v1(1, new)),
        ])
        return carry

    lax.fori_loop(2, 8, step, 0)

    def settled(p):
        return w.deposit(p, *corner(jnp.int32(p))) if p < 4 else w.keep(p, given(p)[1])

    turned = [4, 5, 6, 7, 0, 1, 2, 3]
    run([(w.vp(7), []), ([], w.v3(7)), (w.s3(), w.v5(6)), (w.s3b(4), w.v4()), (w.s4(), w.v4b(4)), (w.s3b(5), w.v5(7))])
    next(chains[0])
    run([(w.s4b(4), w.v4b(5)), (w.s3b(6), w.v5b(4) + settled(4)), (w.s4b(5), w.v4b(6))])
    next(chains[0])
    places = [(given(k)[0], column(given(k)[1])[0]) for k in range(4, 8)]
    outer = (r == 0) | (r == rows - 1)
    middle = []
    for n in range(3, 8):
        old = turned[n - 2]
        run([(w.s3b(turned[n]), w.v5b(old) + settled(old)), (w.s4b(turned[n - 1]), w.v4b(turned[n]))])
        if n == 5:
            for block, into, device in ((0, w.xr, left), (5, w.xl, right)):
                w.merge(places, block, 256, 256)
                middle.append(send(acc.at[:, block, pl.ds(256, 248), :], into.at[:, pl.ds(128, 248), :], device, start=False))

            @pl.when(jnp.logical_not(outer))
            def _():
                for copy in middle:
                    copy.start()

            for block in (0, 5):
                w.merge(places, block, 0, 128)
                w.merge(places, block, 640, 128)
    run([(w.s4b(3), w.v5b(2) + settled(2))])
    run([([], w.v5b(3))])
    next(chains[1])
    next(chains[0])
    run([([], settled(3))])
    next(chains[1])

    @pl.when(outer)
    def _():
        for copy in middle:
            copy.start()

    sides = []
    for block in (0, 5):
        sides.append((send(acc.at[:, block, pl.ds(0, 128), :], w.ybot.at[:, block], up),
                      send(acc.at[:, block, pl.ds(640, 128), :], w.ytop.at[:, block], down)))
    for j in range(1, 5):
        w.merge(places, j, 0, 128)
        w.merge(places, j, 640, 128)
    along = [send(acc.at[:, inner, pl.ds(0, 128), :], w.ybot.at[:, inner], up),
             send(acc.at[:, inner, pl.ds(640, 128), :], w.ytop.at[:, inner], down)]
    for block in (0, 5):
        w.merge(places, block, 128, 128)
        w.merge(places, block, 512, 128)
    corners = []
    for block, got in zip((0, 5), sides):
        arrived(got)
        for row, came, start, size in ((128, w.ytop, 128, 128), (512, w.ybot, 504, 136)):
            for ch in range(2):
                acc[ch, block, row:row + 128] += came[ch, block]
            into, device = (w.xr, left) if block == 0 else (w.xl, right)
            corners.append(send(acc.at[:, block, pl.ds(start, size), :], into.at[:, pl.ds(start - 128, size), :], device))
    next(chains[0])
    for j in range(1, 5):
        w.merge(places, j, 128, 512)
    next(chains[1])
    next(chains[0])
    arrived(along)
    for ch in range(2):
        for j in range(1, 5):
            acc[ch, j, 128:256] += w.ytop[ch, j]
            acc[ch, j, 512:640] += w.ybot[ch, j]
    done = [local(acc.at[:, j, pl.ds(128, 512), :], out.at[:, :, pl.ds(128 * (j - 1), 128)]) for j in (2, 3)]

    def store(h, m):
        return [local(w.full.at[h, m, pl.ds(k * S, S), :], probe_out.at[h, m, :, pl.ds(k * H, H)]) for k in range(2)]

    done += store(core, 0)
    next(chains[1])
    arrived(middle + corners)
    for ch in range(2):
        acc[ch, 1, 128:640] += w.xl[ch]
        acc[ch, 4, 128:640] += w.xr[ch]
    done += [local(acc.at[:, j, pl.ds(128, 512), :], out.at[:, :, pl.ds(128 * (j - 1), 128)]) for j in (1, 4)]
    next(chains[0])
    done += store(1 - core, 0)
    next(chains[1])
    done += store(core, 1)
    next(chains[1])
    done += store(1 - core, 1)
    for copy in done:
        copy.wait()
    send.finish()


def place_kernel(a, b, out_a, out_b, held_a, held_b, sem):
    parts = [((n // 4, pl.ds(128 * (n % 4), 128)), a, held_a, out_a) for n in range(8)]
    parts += [((n // 2, n % 2), b, held_b, out_b) for n in range(4)]
    first = [pltpu.make_async_copy(src.at[at], held.at[at], sem.at[0, n]) for n, (at, src, held, dst) in enumerate(parts)]
    second = [pltpu.make_async_copy(held.at[at], dst.at[at], sem.at[1, n]) for n, (at, src, held, dst) in enumerate(parts)]
    for copy in first:
        copy.start()
    for one, two in zip(first, second):
        one.wait()
        two.start()
    for copy in second:
        copy.wait()


def placed(a, b):
    anywhere = pl.BlockSpec(memory_space=pl.ANY)
    return pl.pallas_call(
        place_kernel,
        out_shape=(jax.ShapeDtypeStruct(a.shape, F32), jax.ShapeDtypeStruct(b.shape, F32)),
        in_specs=[anywhere] * 2,
        out_specs=(anywhere, anywhere),
        scratch_shapes=[pltpu.VMEM(a.shape, F32), pltpu.VMEM(b.shape, F32), pltpu.SemaphoreType.DMA((2, 12))],
        compiler_params=pltpu.CompilerParams(vmem_limit_bytes=60 * 2**20),
    )(a, b)


def body(object_field, probe, patterns, offsets):
    tables_in = [jnp.asarray(t) for t in tables(S)]
    anywhere = pl.BlockSpec(memory_space=pl.ANY)
    return placed(*pl.pallas_call(
        kernel,
        out_shape=(jax.ShapeDtypeStruct(object_field.shape, F32), jax.ShapeDtypeStruct(probe.shape, F32)),
        in_specs=[pl.BlockSpec(memory_space=pltpu.SMEM)] + [anywhere] * 8,
        out_specs=(anywhere, anywhere),
        scratch_shapes=[pltpu.VMEM(*v) for v in SCRATCH.values()] + [
            pltpu.SemaphoreType.DMA((LOCALS,)), pltpu.SemaphoreType.DMA((REMOTES,)), pltpu.SemaphoreType.DMA((REMOTES,))],
        compiler_params=pltpu.CompilerParams(collective_id=0, has_side_effects=True, vmem_limit_bytes=58 * 2**20),
    )(offsets.T, object_field, probe, patterns, *tables_in))


def solution(mesh):
    in_specs = (P(None, "row", "col"), P(), P(("row", "col"), None, None), P(("row", "col"), None))
    out_specs = (P(None, "row", "col"), P())
    return jax.shard_map(body, mesh=mesh, in_specs=in_specs, out_specs=out_specs, check_vma=False)
```
